128 devices in a mesh: prow: 8 (over z, x_lo), pcol: 16 (over x_hi, y, core).
Axes of the slice: x: 4 (x_hi: 2, x_lo: 2; x = x_hi * 2 + x_lo), y: 4, z: 4, core: 2. Of those that a mesh axis runs over, the one named last changes fastest.
Arguments:
- leaf_rhs: float32 [8, 32, 256, 256], P('prow', 'pcol'), may hold values from -6 to 6
- leaf_inverse: float32 [8, 32, 256, 256], P('prow', 'pcol'), as said below
- off_blocks: float32 [8, 2, 8, 32, 512, 256], P('prow', None, None, 'pcol'), may hold values from -0.09375 to 0.09375
- ancestor_rows: int32 [8, 2, 8, 32], P('prow', None, None, 'pcol'), may hold values from 0 to 31
- block_present: int32 [8, 2, 8, 32], P('prow', None, None, 'pcol'), may hold values 0 or 1
- top_rhs: float32 [256, 512, 256], P(('prow', 'pcol')), may hold values from -6 to 6
- top_inverse: float32 [256, 512, 512], P(('prow', 'pcol')), as said below
Outputs:
- leaf_solution: float32 [8, 32, 256, 256], P('prow', 'pcol')
- top_solution: float32 [256, 512, 256], P(('prow', 'pcol'))
The draws below stay inside these ranges and needn't reach their ends.
Inputs may be any that keep to these rules, and one draw needn't show every extreme that they name: `leaf_inverse`: each block is lower triangular with diagonal entries between 1 and 2. `top_inverse`: each block is lower triangular with diagonal entries between 1 and 2.
All inputs are finite; a program needn't handle non-finite values. No bound on the sum of `block_present` on one device may be relied on, other than what follows from the above.
Results may differ from the reference program's by a relative error of at most 0.0001.
Values sent between devices are 32-bit elements; how exact they have to be, the bound alone decides.
A program may use at most 128 MiB of HBM per device.

```python
import math
import jax
import jax.numpy as jnp
from jax import lax

W1 = 256
W2 = 512
RHS = 256
NA = 2
C1C = 2
C2 = 2
SROW = 8
SCOL = 32
GROUPS = 8
GROUP_ROWS = 32
LEVEL2 = 256


def lower_factor(noise, diag_draw, order):
    row_index = lax.broadcasted_iota(jnp.int32, noise.shape, noise.ndim - 2)
    col_index = lax.broadcasted_iota(jnp.int32, noise.shape, noise.ndim - 1)
    below = jnp.where(row_index > col_index, noise * (0.5 / math.sqrt(order)), 0.0)
    return below + jnp.where(row_index == col_index, diag_draw, 0.0)


def draw_leaf_inverse(key, part):
    key = jax.random.fold_in(key, 11)
    first, second = jax.random.split(key)
    shape = (SROW, SCOL, W1, W1)
    noise = jnp.clip(jax.random.normal(first, shape, jnp.float32), -4.0, 4.0)
    diag_draw = jnp.exp(jax.random.uniform(second, shape, jnp.float32, 0.0, 0.693))
    return lower_factor(noise, diag_draw, W1)


def draw_top_inverse(key, part):
    key = jax.random.fold_in(key, 12)
    first, second = jax.random.split(key)
    shape = (LEVEL2, W2, W2)
    noise = jnp.clip(jax.random.normal(first, shape, jnp.float32), -4.0, 4.0)
    diag_draw = jnp.exp(jax.random.uniform(second, shape, jnp.float32, 0.0, 0.693))
    return lower_factor(noise, diag_draw, W2)


def plant(array, own_key, least, high):
    index_at = [jax.random.randint(jax.random.fold_in(own_key, axis), (), 0, length) for axis, length in enumerate(array.shape)]
    longest = array.shape.index(max(array.shape))
    beside = index_at[:longest] + [(index_at[longest] + 1) % array.shape[longest]] + index_at[longest + 1:]
    return array.at[tuple(index_at)].set(least).at[tuple(beside)].set(high)


def levels(rng, shape, cuts, low, largest):
    level, own = 1.0, jax.random.fold_in(rng, 6)
    for dim, shards_of in cuts:
        draws = jnp.exp(jax.random.uniform(jax.random.fold_in(own, dim), (shards_of,), jnp.float32, low / len(cuts), largest / len(cuts)))
        level = level * jnp.repeat(draws, shape[dim] // shards_of).reshape([-1 if axis == dim else 1 for axis in range(len(shape))])
    return level


def normal_values(own_key, dims, scale, bound, cuts=(), dtype=jnp.bfloat16):
    factor_of = levels(own_key, dims, cuts, -0.22, 0.18) if cuts else 1.0
    values = jax.random.normal(own_key, dims, jnp.float32) * scale * factor_of
    return jnp.minimum(jnp.maximum(values, -bound), bound).astype(dtype)


def setup_inputs(seed: int = 0) -> dict:
    key_list = jax.random.split(jax.random.key(seed), 8)
    return {
        "leaf_rhs": normal_values(key_list[0], (SROW, SCOL, W1, RHS), 1.0, 6.0, ((0, 8), (1, 16)), jnp.float32),
        "leaf_inverse": draw_leaf_inverse(jax.random.fold_in(key_list[7], 71), 0),
        "off_blocks": normal_values(key_list[2], (GROUPS, NA, SROW, SCOL, W2, W1), (W1 * NA * SROW * C1C // C2) ** -0.5, 0.09375, ((0, 8), (3, 16)), jnp.float32),
        "ancestor_rows": plant(jax.random.randint(key_list[3], (GROUPS, NA, SROW, SCOL), 0, GROUP_ROWS), jax.random.fold_in(key_list[3], 1), 0, GROUP_ROWS - 1).astype(jnp.int32),
        "block_present": plant((jax.random.randint(key_list[4], (GROUPS, NA, SROW, SCOL), 0, 4) < 3).astype(jnp.int32), jax.random.fold_in(key_list[4], 1), 0, 1),
        "top_rhs": normal_values(key_list[5], (LEVEL2, W2, RHS), 1.0, 6.0, ((0, 128),), jnp.float32),
        "top_inverse": draw_top_inverse(jax.random.fold_in(key_list[7], 71), 0),
    }


def reference(leaf_rhs, leaf_inverse, off_blocks, ancestor_rows, block_present, top_rhs, top_inverse):
    highest = lax.Precision.HIGHEST
    leaf_solution = jnp.einsum("uvij,uvjr->uvir", leaf_inverse, leaf_rhs, precision=highest)

    def one_group(inputs):
        blocks, rows_index, present = inputs

        def one_ancestor(total, inner):
            block_set, index_set, keep_set = inner
            terms = jnp.einsum("uvij,uvjr->uvir", block_set, leaf_solution, precision=highest)
            terms = terms * keep_set.astype(jnp.float32)[:, :, None, None]
            added = jax.ops.segment_sum(terms.reshape(-1, W2, RHS), index_set.reshape(-1), num_segments=GROUP_ROWS)
            return total + added, None

        start = jnp.zeros((GROUP_ROWS, W2, RHS), jnp.float32)
        total, unused = lax.scan(one_ancestor, start, (blocks, rows_index, present))
        return total

    update = lax.map(one_group, (off_blocks, ancestor_rows, block_present)).reshape(LEVEL2, W2, RHS)
    top_solution = jnp.einsum("kij,kjr->kir", top_inverse, top_rhs - update, precision=highest)
    return leaf_solution, top_solution
```

```python
import jax
import jax.numpy as jnp
from jax import lax
from jax.experimental import pallas as pl
from jax.experimental.pallas import tpu as pltpu
from jax.sharding import PartitionSpec as P

MESH = pl.DeviceIdType.MESH
F32, BF16 = jnp.float32, jnp.bfloat16
W1, W2, HALF = 256, 512, 128
STEPS = 8
BUFS = 3
CUT = 288
NONE = 32

UNITS = (
    (1, 2, 0), (1, 2, 1), (0, 2, 0), (0, 2, 1),
    (1, 1, 1), (1, 3, 0), (0, 1, 1), (0, 3, 0),
    (1, 1, 0), (1, 3, 1), (0, 1, 0), (0, 3, 1),
    (1, 0, 0), (1, 0, 1), (0, 0, 0), (0, 0, 1),
)
Y_SEND = ((0, 2, 4, 6, 8, 10), (1, 3, 5, 7, 9, 11))
Y_ADD = ((8, 10, 13, 15, 12, 14), (9, 11, 12, 14, 13, 15))
X_SEND = (0, 1, 4, 5, 8, 9, 12, 13)
XY_SEND = ((2, 6, 10), (3, 7, 11))
XY_ADD = ((10, 15, 14), (11, 14, 15))


def split(value):
    high = value.astype(BF16)
    return high, (value - high.astype(F32)).astype(BF16)


def dot(a, b):
    return jnp.dot(a, b, preferred_element_type=F32)


def times(a_high, a_low, both, high):
    wide = dot(a_high, both)
    return wide[:, :HALF] + wide[:, HALF:] + dot(a_low, high)


def kernel(
    meta, leaf_rhs, leaf_inv, off_blocks, top_rhs, top_inv, leaf_out, top_out,
    x, w, blocks, chain, give, s, yr, xyr, xr, x2r, rhs, inv, inv_high, inv_low,
    block_sem, top_sem, az_s, az_r, ax_s, ax_r, core_s, core_r, y_s, y_r, xy_s, xy_r, x_s, x_r, x2_s, x2_r,
):
    row, col = lax.axis_index("prow"), lax.axis_index("pcol")
    z, xl = row // 2, row % 2
    xh, y, core = col // 8, (col // 2) % 4, col % 2

    def rows_at(dz, dx):
        return ((z + dz) % 4) * 2 + (xl + dx) % 2

    def at(dxh, dy, dcore):
        return ((xh + dxh) % 2) * 8 + ((y + dy) % 4) * 2 + (core + dcore) % 2

    x_near = (rows_at(0, 1), col)
    z_to = ((rows_at(1, 0), col), (rows_at(3, 0), col))
    other_core = (row, at(0, 0, 1))
    x_far = (row, at(1, 0, 0))
    y_to = ((row, at(0, 1, 0)), (row, at(0, 3, 0)))
    order = [rows_at(*d) for d in ((0, 0), (0, 1), (3, 0), (1, 0), (2, 0), (3, 1), (1, 1), (2, 1))]

    def send(src, dst, send_sem, recv_sem, device):
        return pltpu.make_async_remote_copy(
            src_ref=src, dst_ref=dst, send_sem=send_sem, recv_sem=recv_sem, device_id=device, device_id_type=MESH
        )

    def fetch(g):
        u = order[g % STEPS]
        return pltpu.make_async_copy(off_blocks.at[0, :, u], blocks.at[g % BUFS], block_sem.at[g % BUFS])

    for g in range(BUFS):
        fetch(g).start()
    fetch_rhs = pltpu.make_async_copy(top_rhs, rhs, top_sem.at[0])
    fetch_inv = pltpu.make_async_copy(top_inv, inv, top_sem.at[1])
    fetch_rhs.start()
    fetch_inv.start()

    barrier = pltpu.get_barrier_semaphore()
    partners = (x_near, *z_to, other_core, x_far, *y_to)
    for partner in partners:
        pl.semaphore_signal(barrier, inc=1, device_id=partner, device_id_type=MESH)

    chain[NONE] = jnp.zeros((W2, HALF), F32)

    def leaf(ch):
        for v in range(2):
            i_high, i_low = split(leaf_inv[0, v])
            r_high, r_low = split(leaf_rhs[0, v, :, ch * HALF : (ch + 1) * HALF])
            solved = times(i_high, i_low, jnp.concatenate([r_high, r_low], axis=1), r_high)
            x[ch, row, v] = solved
            leaf_out[0, v, :, ch * HALF : (ch + 1) * HALF] = solved

    def x_msg(ch, j, v):
        u = order[0] if j == 0 else order[4]
        ref = x.at[ch, u, v]
        return send(ref, ref, ax_s.at[ch, j, v], ax_r.at[ch, j, v], x_near)

    def z_msg(ch, d, j):
        u = (order[0], order[0], order[2 + d], order[1], order[1])[j]
        v = (d, 1 - d, d, 0, 1)[j]
        ref = x.at[ch, u, v]
        return send(ref, ref, az_s.at[ch, d, j], az_r.at[ch, d, j], z_to[d])

    def gather_own(ch):
        for j in range(2):
            x_msg(ch, 0, j).start()
            for d in range(2):
                z_msg(ch, d, j).start()

    def gather_near(ch):
        for d in range(2):
            z_msg(ch, d, 0).wait_recv()
            z_msg(ch, d, 2).start()
        for j in range(2):
            x_msg(ch, 0, j).wait_recv()
            for d in range(2):
                z_msg(ch, d, 3 + j).start()

    def gather_far(ch):
        for d in range(2):
            z_msg(ch, d, 2).wait_recv()
        for v in range(2):
            x_msg(ch, 1, v).start()

    def gather_wait(ch, step):
        if step in (2, 3):
            z_msg(ch, step - 2, 1).wait_recv()
        if step in (5, 6):
            for j in (3, 4):
                z_msg(ch, step - 5, j).wait_recv()
        if step == 7:
            for v in range(2):
                x_msg(ch, 1, v).wait_recv()

    def gather_sent(ch):
        for d in range(2):
            for j in range(5):
                z_msg(ch, d, j).wait_send()
        for j in range(2):
            for v in range(2):
                x_msg(ch, j, v).wait_send()

    def products(ch, step):
        g = ch * STEPS + step
        u = order[step]
        fetch(g).wait()
        for v in range(2):
            high, low = split(x[ch, u, v])
            w[v, :, :HALF] = high
            w[v, :, HALF:] = low

        def one(i, carry):
            v, a, tile = i // 4, (i // 2) % 2, i % 2
            tall = pl.ds(pl.multiple_of(tile * 256, 256), 256)
            before = meta[a * 16 + u * 2 + v]
            b_high, b_low = split(blocks[g % BUFS, a, v, tall, :])
            term = times(b_high, b_low, w[v], w[v, :, :HALF])
            chain[step * 4 + v * 2 + a, tall, :] = term + chain[before, tall, :]
            return carry

        lax.fori_loop(0, 8, one, 0)
        if g + BUFS < 2 * STEPS:
            fetch(g + BUFS).start()

    def number(i, its_core):
        dxh, dy, e = UNITS[i]
        return ((xh + dxh) % 2) * 16 + ((y + dy) % 4) * 4 + its_core * 2 + e

    def core_msg(ch, i):
        return send(give.at[i], s.at[ch, i], core_s.at[i], core_r.at[ch, i], other_core)

    def y_msg(ch, d, j):
        return send(
            s.at[ch, Y_SEND[d][j], pl.ds(0, CUT)], yr.at[ch, d, j], y_s.at[ch, d, j], y_r.at[ch, d, j], y_to[d]
        )

    def xy_msg(ch, d, j):
        return send(
            s.at[ch, XY_SEND[d][j], pl.ds(CUT, W2 - CUT)],
            xyr.at[ch, d, j],
            xy_s.at[ch, d, j],
            xy_r.at[ch, d, j],
            y_to[d],
        )

    def x_far_msg(ch, m):
        return send(
            s.at[ch, X_SEND[m], pl.ds(CUT, W2 - CUT)], xr.at[ch, m], x_s.at[ch, m], x_r.at[ch, m], x_far
        )

    def x_last_msg(ch, e):
        return send(s.at[ch, 12 + e, pl.ds(0, CUT)], x2r.at[ch, e], x2_s.at[ch, e], x2_r.at[ch, e], x_far)

    def share_core(ch):
        for i in range(16):
            if ch:
                core_msg(ch - 1, i).wait_send()
            give[i] = chain[meta[32 + number(i, 1 - core)]]
            core_msg(ch, i).start()

    def sum_core(ch):
        for i in range(16):
            core_msg(ch, i).wait_recv()
            s[ch, i] = s[ch, i] + chain[meta[32 + number(i, core)]]
            for d in range(2):
                if i in Y_SEND[d][:4]:
                    y_msg(ch, d, Y_SEND[d].index(i)).start()
            if i in X_SEND:
                x_far_msg(ch, X_SEND.index(i)).start()

    def y_add(ch, d, j):
        y_msg(ch, d, j).wait_recv()
        i = Y_ADD[d][j]
        s[ch, i, :CUT] = s[ch, i, :CUT] + yr[ch, d, j]

    def xy_add(ch, d, j):
        xy_msg(ch, d, j).wait_recv()
        i = XY_ADD[d][j]
        s[ch, i, CUT:] = s[ch, i, CUT:] + xyr[ch, d, j]

    def y_pass(ch, j):
        for d in range(2):
            y_add(ch, d, j)
            y_msg(ch, d, 4 + j).start()

    def x_add(ch, m):
        x_far_msg(ch, m).wait_recv()
        i = X_SEND[m] + 2
        s[ch, i, CUT:] = s[ch, i, CUT:] + xr[ch, m]
        for d in range(2):
            if i in XY_SEND[d][:2]:
                xy_msg(ch, d, XY_SEND[d].index(i)).start()

    def xy_pass(ch):
        for d in range(2):
            xy_add(ch, d, 0)
            xy_msg(ch, d, 2).start()

    def y_last(ch):
        for d, j in ((0, 2), (1, 2), (0, 4), (1, 4)):
            y_add(ch, d, j)
        for e in range(2):
            x_last_msg(ch, e).start()

    def finish(ch):
        for d, j in ((0, 3), (1, 3), (0, 5), (1, 5)):
            y_add(ch, d, j)
        for d, j in ((0, 1), (1, 1), (0, 2), (1, 2)):
            xy_add(ch, d, j)
        for e in range(2):
            x_last_msg(ch, e).wait_recv()
            i = 14 + e
            s[ch, i, :CUT] = s[ch, i, :CUT] + x2r[ch, e]
            cols = slice(ch * HALF, (ch + 1) * HALF)
            high, low = split(rhs[e, :, cols] - s[ch, i])
            both = jnp.concatenate([high, low], axis=1)
            top_out[e, :256, cols] = times(
                inv_high[e, :256, :256], inv_low[e, :256, :256], both[:256], high[:256]
            )
            top_out[e, 256:, cols] = times(inv_high[e, 256:], inv_low[e, 256:], both, high)

    leaf(0)
    pl.semaphore_wait(barrier, len(partners))
    gather_own(0)
    leaf(1)
    products(0, 0)
    gather_near(0)
    for step in range(1, 4):
        gather_wait(0, step)
        products(0, step)
    gather_far(0)
    for step in range(4, 8):
        gather_wait(0, step)
        products(0, step)
    gather_own(1)
    share_core(0)
    sum_core(0)
    gather_near(1)

    fetch_rhs.wait()
    fetch_inv.wait()

    def split_inv(i, carry):
        e, tall = i // 4, pl.ds(pl.multiple_of((i % 4) * 128, 128), 128)
        high, low = split(inv[e, tall, :])
        inv_high[e, tall, :] = high
        inv_low[e, tall, :] = low
        return carry

    lax.fori_loop(0, 8, split_inv, 0)

    for step in range(0, 2):
        products(1, step)
    y_pass(0, 0)
    for step in range(2, 4):
        gather_wait(1, step)
        products(1, step)
    gather_far(1)
    y_pass(0, 1)
    for step in range(4, 8):
        gather_wait(1, step)
        products(1, step)
    share_core(1)
    sum_core(1)
    for m in range(8):
        x_add(0, m)
    xy_pass(0)
    y_last(0)
    y_pass(1, 0)
    y_pass(1, 1)
    finish(0)
    for m in range(8):
        x_add(1, m)
    xy_pass(1)
    y_last(1)
    finish(1)

    for ch in range(2):
        gather_sent(ch)
        for d in range(2):
            for j in range(6):
                y_msg(ch, d, j).wait_send()
            for j in range(3):
                xy_msg(ch, d, j).wait_send()
        for m in range(8):
            x_far_msg(ch, m).wait_send()
        for e in range(2):
            x_last_msg(ch, e).wait_send()
    for i in range(16):
        core_msg(1, i).wait_send()


def chains(rows_index, present, row):
    u = lax.broadcasted_iota(jnp.int32, (2, 8, 2), 1)
    a = lax.broadcasted_iota(jnp.int32, (2, 8, 2), 0)
    v = lax.broadcasted_iota(jnp.int32, (2, 8, 2), 2)
    far = (u // 2 - row // 2 + 4) % 4
    near = (u + row) % 2
    step = jnp.where(
        far == 0, near, jnp.where(far == 3, 2 + 3 * near, jnp.where(far == 1, 3 + 3 * near, 4 + 3 * near))
    )
    rank = (step * 4 + v * 2 + a).reshape(-1)
    wanted = jnp.where(present != 0, rows_index, -1).reshape(-1)
    ask = jnp.concatenate([wanted, jnp.arange(32, dtype=jnp.int32)])
    limit = jnp.concatenate([rank, jnp.full((32,), 32, jnp.int32)])
    fits = (wanted[None, :] == ask[:, None]) & (rank[None, :] < limit[:, None])
    found = jnp.max(jnp.where(fits, rank[None, :], -1), axis=1)
    return jnp.where(found < 0, NONE, found)


def per_device(leaf_rhs, leaf_inverse, off_blocks, ancestor_rows, block_present, top_rhs, top_inverse):
    meta = chains(ancestor_rows[0], block_present[0], lax.axis_index("prow"))
    vmem = pl.BlockSpec(memory_space=pltpu.VMEM)
    smem = pl.BlockSpec(memory_space=pltpu.SMEM)
    anywhere = pl.BlockSpec(memory_space=pl.ANY)
    rest = W2 - CUT
    dma = pltpu.SemaphoreType.DMA
    return pl.pallas_call(
        kernel,
        out_shape=(
            jax.ShapeDtypeStruct(leaf_rhs.shape, F32),
            jax.ShapeDtypeStruct(top_rhs.shape, F32),
        ),
        in_specs=[smem, vmem, vmem, anywhere, anywhere, anywhere],
        out_specs=(vmem, vmem),
        scratch_shapes=[
            pltpu.VMEM((2, 8, 2, W1, HALF), F32),
            pltpu.VMEM((2, W1, 2 * HALF), BF16),
            pltpu.VMEM((BUFS, 2, 2, W2, W1), F32),
            pltpu.VMEM((NONE + 1, W2, HALF), F32),
            pltpu.VMEM((16, W2, HALF), F32),
            pltpu.VMEM((2, 16, W2, HALF), F32),
            pltpu.VMEM((2, 2, 6, CUT, HALF), F32),
            pltpu.VMEM((2, 2, 3, rest, HALF), F32),
            pltpu.VMEM((2, 8, rest, HALF), F32),
            pltpu.VMEM((2, 2, CUT, HALF), F32),
            pltpu.VMEM((2, W2, 2 * HALF), F32),
            pltpu.VMEM((2, W2, W2), F32),
            pltpu.VMEM((2, W2, W2), BF16),
            pltpu.VMEM((2, W2, W2), BF16),
            dma((BUFS,)),
            dma((2,)),
            dma((2, 2, 5)),
            dma((2, 2, 5)),
            dma((2, 2, 2)),
            dma((2, 2, 2)),
            dma((16,)),
            dma((2, 16)),
            dma((2, 2, 6)),
            dma((2, 2, 6)),
            dma((2, 2, 3)),
            dma((2, 2, 3)),
            dma((2, 8)),
            dma((2, 8)),
            dma((2, 2)),
            dma((2, 2)),
        ],
        compiler_params=pltpu.CompilerParams(
            collective_id=0, has_side_effects=True, vmem_limit_bytes=60 * 1024 * 1024
        ),
        cost_estimate=pl.CostEstimate(flops=7_500_000_000, bytes_accessed=40_000_000, transcendentals=0),
    )(meta, leaf_rhs, leaf_inverse, off_blocks, top_rhs, top_inverse)


def solution(mesh):
    return jax.shard_map(
        per_device,
        mesh=mesh,
        in_specs=(
            P("prow", "pcol", None, None),
            P("prow", "pcol", None, None),
            P("prow", None, None, "pcol", None, None),
            P("prow", None, None, "pcol"),
            P("prow", None, None, "pcol"),
            P(("prow", "pcol"), None, None),
            P(("prow", "pcol"), None, None),
        ),
        out_specs=(P("prow", "pcol", None, None), P(("prow", "pcol"), None, None)),
        check_vma=False,
    )
```

```python
import jax
import jax.numpy as jnp
from jax import lax
from jax.experimental import pallas as pl
from jax.experimental.pallas import tpu as pltpu
from jax.sharding import PartitionSpec as P

MESH = pl.DeviceIdType.MESH
F32, BF16 = jnp.float32, jnp.bfloat16
W1, W2, HALF = 256, 512, 128
STEPS = 8
BUFS = 3
CUT = 288
NONE = 32

UNITS = (
    (1, 2, 0), (1, 2, 1), (0, 2, 0), (0, 2, 1),
    (1, 1, 1), (1, 3, 0), (0, 1, 1), (0, 3, 0),
    (1, 1, 0), (1, 3, 1), (0, 1, 0), (0, 3, 1),
    (1, 0, 0), (1, 0, 1), (0, 0, 0), (0, 0, 1),
)
Y_SEND = ((0, 2, 4, 6, 8, 10), (1, 3, 5, 7, 9, 11))
Y_ADD = ((8, 10, 13, 15, 12, 14), (9, 11, 12, 14, 13, 15))
X_SEND = (0, 1, 4, 5, 8, 9, 12, 13)
XY_SEND = ((2, 6, 10), (3, 7, 11))
XY_ADD = ((10, 15, 14), (11, 14, 15))


ORDER = (
    ("leaf", 0), ("own", 0), ("leaf", 1), ("p", 0, 0), ("inv",), ("zpass", 0, 0), ("zpass", 0, 1), ("near", 0, 0),
    ("near", 0, 1), ("p", 0, 1), ("p", 0, 2), ("p", 0, 3), ("far", 0), ("own", 1), ("p", 0, 4), ("p", 0, 5),
    ("p", 0, 6), ("p", 0, 7), ("zpass", 1, 0), ("zpass", 1, 1), ("give", 0, 0), ("give", 0, 1), ("give", 0, 2),
    ("give", 0, 3), ("give", 0, 4), ("give", 0, 5), ("give", 0, 6), ("give", 0, 7), ("give", 0, 8), ("give", 0, 9),
    ("give", 0, 10), ("give", 0, 11), ("give", 0, 12), ("give", 0, 13), ("give", 0, 14), ("near", 1, 0),
    ("give", 0, 15), ("sum", 0, 0), ("sum", 0, 1), ("sum", 0, 2), ("sum", 0, 3), ("near", 1, 1), ("sum", 0, 4),
    ("sum", 0, 5), ("sum", 0, 6), ("sum", 0, 7), ("sum", 0, 8), ("sum", 0, 9), ("xadd", 0, 0), ("far", 1, 0),
    ("sum", 0, 10), ("ypass", 0, 0, 0), ("sum", 0, 11), ("ypass", 0, 1, 0), ("sum", 0, 12), ("sum", 0, 13),
    ("xadd", 0, 1), ("sum", 0, 14), ("sum", 0, 15), ("far", 1, 1), ("p", 1, 0), ("ypass", 0, 0, 1), ("p", 1, 1),
    ("ypass", 0, 1, 1), ("xadd", 0, 2), ("p", 1, 2), ("p", 1, 3), ("xadd", 0, 3), ("p", 1, 4), ("p", 1, 5),
    ("xadd", 0, 4), ("p", 1, 6), ("p", 1, 7), ("give", 1, 0), ("give", 1, 1), ("xadd", 0, 5), ("give", 1, 2),
    ("give", 1, 3), ("xypass", 0, 0), ("give", 1, 4), ("give", 1, 5), ("give", 1, 6), ("give", 1, 7), ("give", 1, 8),
    ("give", 1, 9), ("give", 1, 10), ("give", 1, 11), ("give", 1, 12), ("give", 1, 13), ("ylast", 0, 1),
    ("give", 1, 14), ("give", 1, 15), ("xadd", 0, 6), ("sum", 1, 0), ("sum", 1, 1), ("ylast", 0, 0), ("sum", 1, 2),
    ("xypass", 0, 1), ("sum", 1, 3), ("sum", 1, 4), ("xadd", 0, 7), ("sum", 1, 5), ("sum", 1, 6), ("sum", 1, 7),
    ("sum", 1, 8), ("sum", 1, 9), ("sum", 1, 10), ("sum", 1, 11), ("sum", 1, 12), ("sum", 1, 13), ("sum", 1, 14),
    ("sum", 1, 15), ("xadd", 1, 0), ("ypass", 1, 1, 0), ("xadd", 1, 1), ("ypass", 1, 0, 0), ("fin", 0, 1),
    ("fin", 0, 0), ("ypass", 1, 0, 1), ("ypass", 1, 1, 1), ("xadd", 1, 2), ("xadd", 1, 3), ("xadd", 1, 4),
    ("xadd", 1, 5), ("xypass", 1, 0), ("ylast", 1, 1), ("xadd", 1, 6), ("ylast", 1, 0), ("xypass", 1, 1),
    ("xadd", 1, 7), ("fin", 1, 0), ("fin", 1, 1),
)


def split(value):
    high = value.astype(BF16)
    return high, (value - high.astype(F32)).astype(BF16)


def dot(a, b):
    return jnp.dot(a, b, preferred_element_type=F32)


def times(a_high, a_low, both, high):
    wide = dot(a_high, both)
    return wide[:, :HALF] + wide[:, HALF:] + dot(a_low, high)


def kernel(
    meta, leaf_rhs, leaf_inv, off_blocks, top_rhs, top_inv, leaf_out, top_out,
    x, w, blocks, chain, give, s, yr, xyr, xr, x2r, rhs, inv, inv_high, inv_low,
    block_sem, top_sem, az_s, az_r, ax_s, ax_r, core_s, core_r, y_s, y_r, xy_s, xy_r, x_s, x_r, x2_s, x2_r,
):
    row, col = lax.axis_index("prow"), lax.axis_index("pcol")
    z, xl = row // 2, row % 2
    xh, y, core = col // 8, (col // 2) % 4, col % 2

    def rows_at(dz, dx):
        return ((z + dz) % 4) * 2 + (xl + dx) % 2

    def at(dxh, dy, dcore):
        return ((xh + dxh) % 2) * 8 + ((y + dy) % 4) * 2 + (core + dcore) % 2

    x_near = (rows_at(0, 1), col)
    z_to = ((rows_at(1, 0), col), (rows_at(3, 0), col))
    other_core = (row, at(0, 0, 1))
    x_far = (row, at(1, 0, 0))
    y_to = ((row, at(0, 1, 0)), (row, at(0, 3, 0)))
    order = [rows_at(*d) for d in ((0, 0), (0, 1), (3, 0), (1, 0), (2, 0), (3, 1), (1, 1), (2, 1))]

    def send(src, dst, send_sem, recv_sem, device):
        return pltpu.make_async_remote_copy(
            src_ref=src, dst_ref=dst, send_sem=send_sem, recv_sem=recv_sem, device_id=device, device_id_type=MESH
        )

    def fetch(g):
        u = order[g % STEPS]
        return pltpu.make_async_copy(off_blocks.at[0, :, u], blocks.at[g % BUFS], block_sem.at[g % BUFS])

    for g in range(BUFS):
        fetch(g).start()
    fetch_rhs = pltpu.make_async_copy(top_rhs, rhs, top_sem.at[0])
    fetch_inv = pltpu.make_async_copy(top_inv, inv, top_sem.at[1])
    fetch_rhs.start()
    fetch_inv.start()

    barrier = pltpu.get_barrier_semaphore()
    partners = (x_near, *z_to, other_core, x_far, *y_to)
    for partner in partners:
        pl.semaphore_signal(barrier, inc=1, device_id=partner, device_id_type=MESH)

    chain[NONE] = jnp.zeros((W2, HALF), F32)

    started, seen = {}, set()

    def put(key):
        started[key] = message(*key)
        started[key].start()

    def need(*keys):
        for key in keys:
            if key not in seen:
                seen.add(key)
                message(*key).wait_recv()

    def message(kind, ch, j, k=0):
        low, high = pl.ds(0, CUT), pl.ds(CUT, W2 - CUT)
        if kind == "near":
            ref = x.at[ch, order[0] if j == 0 else order[4], k]
            return send(ref, ref, ax_s.at[ch, j, k], ax_r.at[ch, j, k], x_near)
        if kind == "z":
            u = (order[0], order[0], order[2 + j], order[1], order[1], order[5 + j])[k]
            ref = x.at[ch, u, (j, 1 - j, j, 0, 1, j)[k]]
            return send(ref, ref, az_s.at[ch, j, k], az_r.at[ch, j, k], z_to[j])
        if kind == "core":
            return send(give.at[j], s.at[ch, j], core_s.at[j], core_r.at[ch, j], other_core)
        if kind == "y":
            return send(s.at[ch, Y_SEND[j][k], low], yr.at[ch, j, k], y_s.at[ch, j, k], y_r.at[ch, j, k], y_to[j])
        if kind == "xy":
            return send(s.at[ch, XY_SEND[j][k], high], xyr.at[ch, j, k], xy_s.at[ch, j, k], xy_r.at[ch, j, k], y_to[j])
        if kind == "x":
            return send(s.at[ch, X_SEND[j], high], xr.at[ch, j], x_s.at[ch, j], x_r.at[ch, j], x_far)
        return send(s.at[ch, 12 + j, low], x2r.at[ch, j], x2_s.at[ch, j], x2_r.at[ch, j], x_far)

    def leaf(ch):
        cols = slice(ch * HALF, (ch + 1) * HALF)
        for v in range(2):
            i_high, i_low = split(leaf_inv[0, v])
            r_high, r_low = split(leaf_rhs[0, v, :, cols])
            solved = times(i_high, i_low, jnp.concatenate([r_high, r_low], axis=1), r_high)
            x[ch, row, v] = solved
            leaf_out[0, v, :, cols] = solved

    def own(ch):
        if ch == 0:
            pl.semaphore_wait(barrier, len(partners))
        for j in range(2):
            put(("near", ch, 0, j))
            for d in range(2):
                put(("z", ch, d, j))

    def zpass(ch, d):
        need(("z", ch, d, 0))
        put(("z", ch, d, 2))

    def near(ch, j):
        need(("near", ch, 0, j))
        for d in range(2):
            put(("z", ch, d, 3 + j))

    def far(ch, d=0):
        if ch == 0:
            need(("z", ch, 0, 2), ("z", ch, 1, 2))
            for v in range(2):
                put(("near", ch, 1, v))
        else:
            need(("z", ch, d, 3 + d))
            put(("z", ch, d, 5))

    def products(ch, step):
        last = [("near", 0, 1, 0), ("near", 0, 1, 1)] if ch == 0 else [("z", 1, 0, 5), ("z", 1, 1, 5)]
        need(
            *(
                [],
                [("near", ch, 0, 0), ("near", ch, 0, 1)],
                [("z", ch, 0, 0), ("z", ch, 0, 1)],
                [("z", ch, 1, 0), ("z", ch, 1, 1)],
                [("z", ch, 0, 2), ("z", ch, 1, 2)],
                [("z", ch, 0, 3), ("z", ch, 0, 4)],
                [("z", ch, 1, 3), ("z", ch, 1, 4)],
                last,
            )[step]
        )
        g = ch * STEPS + step
        u = order[step]
        fetch(g).wait()
        for v in range(2):
            high, low = split(x[ch, u, v])
            w[v, :, :HALF] = high
            w[v, :, HALF:] = low

        def one(v, carry):
            for a in range(2):
                before = meta[a * 16 + u * 2 + v]
                for tile in range(2):
                    tall = slice(tile * 256, tile * 256 + 256)
                    b_high, b_low = split(blocks[g % BUFS, a, v, tall, :])
                    term = times(b_high, b_low, w[v], w[v, :, :HALF])
                    chain[step * 4 + v * 2 + a, tall, :] = term + chain[before, tall, :]
            return carry

        lax.fori_loop(0, 2, one, 0)
        if g + BUFS < 2 * STEPS:
            fetch(g + BUFS).start()

    def number(i, its_core):
        dxh, dy, e = UNITS[i]
        return ((xh + dxh) % 2) * 16 + ((y + dy) % 4) * 4 + its_core * 2 + e

    def share_core(ch, i):
        if ch:
            started.pop(("core", 0, i)).wait_send()
        give[i] = chain[meta[32 + number(i, 1 - core)]]
        put(("core", ch, i))

    def sum_core(ch, i):
        need(("core", ch, i))
        s[ch, i] = s[ch, i] + chain[meta[32 + number(i, core)]]
        for d in range(2):
            if i in Y_SEND[d][:4]:
                put(("y", ch, d, Y_SEND[d].index(i)))
        if i in X_SEND:
            put(("x", ch, X_SEND.index(i)))

    def y_add(ch, i, least):
        for d in range(2):
            for j in range(least, 6):
                if Y_ADD[d][j] == i:
                    need(("y", ch, d, j))
                    s[ch, i, :CUT] = s[ch, i, :CUT] + yr[ch, d, j]

    def y_pass(ch, d, j):
        need(("y", ch, d, j))
        i = Y_ADD[d][j]
        s[ch, i, :CUT] = s[ch, i, :CUT] + yr[ch, d, j]
        put(("y", ch, d, 4 + j))

    def x_add(ch, m):
        need(("x", ch, m))
        i = X_SEND[m] + 2
        s[ch, i, CUT:] = s[ch, i, CUT:] + xr[ch, m]
        for d in range(2):
            if i in XY_SEND[d][:2]:
                put(("xy", ch, d, XY_SEND[d].index(i)))

    def xy_pass(ch, d):
        need(("xy", ch, d, 0))
        i = XY_ADD[d][0]
        s[ch, i, CUT:] = s[ch, i, CUT:] + xyr[ch, d, 0]
        put(("xy", ch, d, 2))

    def y_last(ch, e):
        y_add(ch, 12 + e, 2)
        put(("last", ch, e))

    def split_inv():
        fetch_rhs.wait()
        fetch_inv.wait()

        def one(i, carry):
            e, tall = i // 4, pl.ds(pl.multiple_of((i % 4) * 128, 128), 128)
            high, low = split(inv[e, tall, :])
            inv_high[e, tall, :] = high
            inv_low[e, tall, :] = low
            return carry

        lax.fori_loop(0, 8, one, 0)

    def finish(ch, e):
        i = 14 + e
        y_add(ch, i, 2)
        for d in range(2):
            for j in (1, 2):
                if XY_ADD[d][j] == i:
                    need(("xy", ch, d, j))
                    s[ch, i, CUT:] = s[ch, i, CUT:] + xyr[ch, d, j]
        need(("last", ch, e))
        s[ch, i, :CUT] = s[ch, i, :CUT] + x2r[ch, e]
        cols = slice(ch * HALF, (ch + 1) * HALF)
        high, low = split(rhs[e, :, cols] - s[ch, i])
        both = jnp.concatenate([high, low], axis=1)
        top_out[e, :256, cols] = times(inv_high[e, :256, :256], inv_low[e, :256, :256], both[:256], high[:256])
        top_out[e, 256:, cols] = times(inv_high[e, 256:], inv_low[e, 256:], both, high)

    tasks = {
        "leaf": leaf, "own": own, "zpass": zpass, "near": near, "far": far, "p": products, "inv": split_inv,
        "give": share_core, "sum": sum_core, "ypass": y_pass, "xadd": x_add, "xypass": xy_pass,
        "ylast": y_last, "fin": finish,
    }
    for name, *numbers in ORDER:
        tasks[name](*numbers)
    for copy in started.values():
        copy.wait_send()


def hand_over(leaf_in, top_in, leaf_out, top_out, leaf, top, sem):
    pieces = [(ref.at[0, v], held.at[0, v], out.at[0, v]) for ref, held, out in ((leaf_in, leaf, leaf_out),) for v in range(2)]
    pieces += [
        (top_in.at[e, half], top.at[e, half], top_out.at[e, half])
        for e in range(2)
        for half in (pl.ds(0, 256), pl.ds(256, 256))
    ]
    loads = [pltpu.make_async_copy(src, held, sem.at[0, i]) for i, (src, held, _) in enumerate(pieces)]
    stores = [pltpu.make_async_copy(held, out, sem.at[1, i]) for i, (_, held, out) in enumerate(pieces)]
    for load in loads:
        load.start()
    for load, store in zip(loads, stores):
        load.wait()
        store.start()
    for store in stores:
        store.wait()


def chains(rows_index, present, row):
    u = lax.broadcasted_iota(jnp.int32, (2, 8, 2), 1)
    a = lax.broadcasted_iota(jnp.int32, (2, 8, 2), 0)
    v = lax.broadcasted_iota(jnp.int32, (2, 8, 2), 2)
    far = (u // 2 - row // 2 + 4) % 4
    near = (u + row) % 2
    step = jnp.where(
        far == 0, near, jnp.where(far == 3, 2 + 3 * near, jnp.where(far == 1, 3 + 3 * near, 4 + 3 * near))
    )
    rank = (step * 4 + v * 2 + a).reshape(-1)
    wanted = jnp.where(present != 0, rows_index, -1).reshape(-1)
    ask = jnp.concatenate([wanted, jnp.arange(32, dtype=jnp.int32)])
    limit = jnp.concatenate([rank, jnp.full((32,), 32, jnp.int32)])
    fits = (wanted[None, :] == ask[:, None]) & (rank[None, :] < limit[:, None])
    found = jnp.max(jnp.where(fits, rank[None, :], -1), axis=1)
    return jnp.where(found < 0, NONE, found)


def per_device(leaf_rhs, leaf_inverse, off_blocks, ancestor_rows, block_present, top_rhs, top_inverse):
    meta = chains(ancestor_rows[0], block_present[0], lax.axis_index("prow"))
    vmem = pl.BlockSpec(memory_space=pltpu.VMEM)
    smem = pl.BlockSpec(memory_space=pltpu.SMEM)
    anywhere = pl.BlockSpec(memory_space=pl.ANY)
    rest = W2 - CUT
    dma = pltpu.SemaphoreType.DMA
    leaf, top = pl.pallas_call(
        kernel,
        out_shape=(
            jax.ShapeDtypeStruct(leaf_rhs.shape, F32),
            jax.ShapeDtypeStruct(top_rhs.shape, F32),
        ),
        in_specs=[smem, vmem, vmem, anywhere, anywhere, anywhere],
        out_specs=(vmem, vmem),
        scratch_shapes=[
            pltpu.VMEM((2, 8, 2, W1, HALF), F32),
            pltpu.VMEM((2, W1, 2 * HALF), BF16),
            pltpu.VMEM((BUFS, 2, 2, W2, W1), F32),
            pltpu.VMEM((NONE + 1, W2, HALF), F32),
            pltpu.VMEM((16, W2, HALF), F32),
            pltpu.VMEM((2, 16, W2, HALF), F32),
            pltpu.VMEM((2, 2, 6, CUT, HALF), F32),
            pltpu.VMEM((2, 2, 3, rest, HALF), F32),
            pltpu.VMEM((2, 8, rest, HALF), F32),
            pltpu.VMEM((2, 2, CUT, HALF), F32),
            pltpu.VMEM((2, W2, 2 * HALF), F32),
            pltpu.VMEM((2, W2, W2), F32),
            pltpu.VMEM((2, W2, W2), BF16),
            pltpu.VMEM((2, W2, W2), BF16),
            dma((BUFS,)),
            dma((2,)),
            dma((2, 2, 6)),
            dma((2, 2, 6)),
            dma((2, 2, 2)),
            dma((2, 2, 2)),
            dma((16,)),
            dma((2, 16)),
            dma((2, 2, 6)),
            dma((2, 2, 6)),
            dma((2, 2, 3)),
            dma((2, 2, 3)),
            dma((2, 8)),
            dma((2, 8)),
            dma((2, 2)),
            dma((2, 2)),
        ],
        compiler_params=pltpu.CompilerParams(
            collective_id=0, has_side_effects=True, vmem_limit_bytes=60 * 1024 * 1024
        ),
        cost_estimate=pl.CostEstimate(flops=7_500_000_000, bytes_accessed=40_000_000, transcendentals=0),
    )(meta, leaf_rhs, leaf_inverse, off_blocks, top_rhs, top_inverse)
    return pl.pallas_call(
        hand_over,
        out_shape=(jax.ShapeDtypeStruct(leaf_rhs.shape, F32), jax.ShapeDtypeStruct(top_rhs.shape, F32)),
        in_specs=[anywhere, anywhere],
        out_specs=(anywhere, anywhere),
        scratch_shapes=[pltpu.VMEM(leaf_rhs.shape, F32), pltpu.VMEM(top_rhs.shape, F32), dma((2, 6))],
    )(leaf, top)


def solution(mesh):
    return jax.shard_map(
        per_device,
        mesh=mesh,
        in_specs=(
            P("prow", "pcol", None, None),
            P("prow", "pcol", None, None),
            P("prow", None, None, "pcol", None, None),
            P("prow", None, None, "pcol"),
            P("prow", None, None, "pcol"),
            P(("prow", "pcol"), None, None),
            P(("prow", "pcol"), None, None),
        ),
        out_specs=(P("prow", "pcol", None, None), P(("prow", "pcol"), None, None)),
        check_vma=False,
    )
```

```python
import jax
import jax.numpy as jnp
from jax import lax
from jax.experimental import pallas as pl
from jax.experimental.pallas import tpu as pltpu
from jax.sharding import PartitionSpec as P

MESH = pl.DeviceIdType.MESH
F32, BF16 = jnp.float32, jnp.bfloat16
W1, W2, HALF = 256, 512, 128
STEPS = 8
BUFS = 3
CUT = 320
REST = W2 - CUT
NONE = 32
PACKED = (True, True, False)
PARTS = len(PACKED)
NARROW = tuple(c for c in range(PARTS) if PACKED[c])
CHAINS = 2
FAR_BY_Z = (False, True, True)

UNITS = (
    (1, 2, 0), (1, 2, 1), (0, 2, 0), (0, 2, 1),
    (1, 1, 1), (1, 3, 0), (0, 1, 1), (0, 3, 0),
    (1, 1, 0), (1, 3, 1), (0, 1, 0), (0, 3, 1),
    (1, 0, 0), (1, 0, 1), (0, 0, 0), (0, 0, 1),
)
PAIRS = ((1, 2), (0, 2), (1, 1), (1, 3), (0, 1), (0, 3), (1, 0), (0, 0))
Y_SEND = ((0, 2, 4, 6, 8, 10), (1, 3, 5, 7, 9, 11))
Y_ADD = ((8, 10, 13, 15, 12, 14), (9, 11, 12, 14, 13, 15))
X_SEND = (0, 1, 4, 5, 8, 9, 12, 13)
XY_SEND = ((2, 6, 10), (3, 7, 11))
XY_ADD = ((10, 15, 14), (11, 14, 15))


ORDER = (
    ("leaf", 0), ("own", 0), ("chains",), ("leaf", 2), ("p", 0, 0), ("inv",), ("zpass", 0, 0), ("zpass", 0, 1),
    ("near", 0, 0), ("near", 0, 1), ("p", 0, 1), ("p", 0, 2), ("far", 0, 0), ("far", 0, 1), ("own", 1), ("p", 0, 3),
    ("p", 0, 4), ("p", 0, 5), ("p", 0, 6), ("zpass", 1, 1), ("zpass", 1, 0), ("p", 0, 7), ("give", 0, 0),
    ("give", 0, 1), ("give", 0, 2), ("near", 1, 0), ("give", 0, 3), ("give", 0, 4), ("p", 1, 0), ("near", 1, 1),
    ("p", 1, 1), ("sum", 0, 0), ("p", 1, 2), ("far", 1, 0), ("sum", 0, 1), ("p", 1, 3), ("far", 1, 1), ("own", 2),
    ("sum", 0, 2), ("sum", 0, 3), ("sum", 0, 4), ("give", 0, 5), ("give", 0, 6), ("give", 0, 7), ("xadd", 0, 0),
    ("p", 1, 4), ("p", 1, 5), ("ypass", 0, 0, 1), ("xadd", 0, 1), ("ypass", 0, 0, 0), ("sum", 0, 5),
    ("ypass", 0, 1, 1), ("p", 1, 6), ("p", 1, 7), ("give", 1, 0), ("sum", 0, 6), ("sum", 0, 7), ("near", 2, 0),
    ("p", 2, 0), ("give", 1, 1), ("give", 1, 2), ("zpass", 2, 0), ("ypass", 0, 1, 0), ("p", 2, 1), ("xadd", 0, 2),
    ("near", 2, 1), ("sum", 1, 0), ("give", 1, 3), ("zpass", 2, 1), ("p", 2, 2), ("sum", 1, 1), ("p", 2, 3),
    ("xadd", 0, 3), ("xadd", 0, 4), ("xypass", 0, 0), ("far", 2, 0), ("ylast", 0, 1), ("xadd", 0, 5),
    ("xypass", 0, 1), ("ylast", 0, 0), ("sum", 1, 2), ("sum", 1, 3), ("give", 1, 4), ("give", 1, 5), ("give", 1, 6),
    ("give", 1, 7), ("xadd", 0, 6), ("ypass", 1, 1, 0), ("ypass", 1, 0, 0), ("xadd", 0, 7), ("far", 2, 1),
    ("xadd", 1, 0), ("sum", 1, 4), ("ypass", 1, 0, 1), ("sum", 1, 5), ("xadd", 1, 1), ("ypass", 1, 1, 1),
    ("sum", 1, 6), ("sum", 1, 7), ("p", 2, 4), ("p", 2, 5), ("p", 2, 6), ("p", 2, 7), ("give", 2, 0),
    ("ylast", 1, 1), ("xadd", 1, 2), ("xadd", 1, 4), ("xypass", 1, 0), ("give", 2, 1), ("give", 2, 2),
    ("give", 2, 3), ("give", 2, 4), ("give", 2, 5), ("fin", 0, 0), ("xadd", 1, 3), ("give", 2, 6), ("give", 2, 7),
    ("give", 2, 8), ("give", 2, 9), ("give", 2, 10), ("give", 2, 11), ("give", 2, 12), ("give", 2, 13),
    ("give", 2, 14), ("give", 2, 15), ("xadd", 1, 5), ("xypass", 1, 1), ("ylast", 1, 0), ("sum", 2, 0),
    ("fin", 0, 1), ("xadd", 1, 6), ("sum", 2, 1), ("sum", 2, 2), ("sum", 2, 3), ("xadd", 1, 7), ("sum", 2, 4),
    ("sum", 2, 5), ("sum", 2, 6), ("fin", 1, 1), ("sum", 2, 7), ("sum", 2, 8), ("sum", 2, 9), ("fin", 1, 0),
    ("sum", 2, 10), ("top", 0, 1), ("ypass", 2, 0, 0), ("sum", 2, 11), ("sum", 2, 12), ("top", 0, 0),
    ("ypass", 2, 1, 0), ("sum", 2, 13), ("sum", 2, 14), ("xadd", 2, 0), ("sum", 2, 15), ("xadd", 2, 1),
    ("ypass", 2, 0, 1), ("ypass", 2, 1, 1), ("xadd", 2, 2), ("xadd", 2, 3), ("xadd", 2, 4), ("xadd", 2, 5),
    ("xadd", 2, 6), ("ylast", 2, 0), ("ylast", 2, 1), ("xadd", 2, 7), ("xypass", 2, 0), ("xypass", 2, 1),
    ("fin", 2, 0), ("top", 1, 0), ("fin", 2, 1), ("top", 1, 1),
)

def split(value):
    high = value.astype(BF16)
    return high, (value - high.astype(F32)).astype(BF16)


def dot(a, b):
    return jnp.dot(a, b, preferred_element_type=F32)


def times(a_high, a_low, both, high):
    wide = dot(a_high, both)
    return wide[:, :HALF] + wide[:, HALF:] + dot(a_low, high)


def kernel(
    wanted, leaf_rhs_in, leaf_inv_in, off_blocks, top_rhs, top_inv, leaf_to, top_to,
    leaf_rhs, leaf_inv, leaf_out, top_out, found, meta,
    x_wide, x_pack, w, blocks, chain, give, s_wide, s_pack, y_wide, y_pack, xy_wide, xy_pack, far_wide, far_pack,
    last_wide, last_pack, rhs, inv, inv_high, inv_low,
    block_sem, top_sem, leaf_sem, out_sem, meta_sem, az_s, az_r, ax_s, ax_r, core_s, core_r, y_s, y_r, xy_s, xy_r, x_s, x_r, x2_s, x2_r,
):
    row, col = lax.axis_index("prow"), lax.axis_index("pcol")
    z, xl = row // 2, row % 2
    xh, y, core = col // 8, (col // 2) % 4, col % 2

    def rows_at(dz, dx):
        return ((z + dz) % 4) * 2 + (xl + dx) % 2

    def at(dxh, dy, dcore):
        return ((xh + dxh) % 2) * 8 + ((y + dy) % 4) * 2 + (core + dcore) % 2

    x_near = (rows_at(0, 1), col)
    z_to = ((rows_at(1, 0), col), (rows_at(3, 0), col))
    other_core = (row, at(0, 0, 1))
    x_far = (row, at(1, 0, 0))
    y_to = ((row, at(0, 1, 0)), (row, at(0, 3, 0)))
    order = [rows_at(*d) for d in ((0, 0), (0, 1), (3, 0), (1, 0), (2, 0), (3, 1), (1, 1), (2, 1))]

    def send(src, dst, send_sem, recv_sem, device):
        return pltpu.make_async_remote_copy(
            src_ref=src, dst_ref=dst, send_sem=send_sem, recv_sem=recv_sem, device_id=device, device_id_type=MESH
        )

    def fetch(g):
        u = order[g % STEPS]
        return pltpu.make_async_copy(off_blocks.at[0, :, u], blocks.at[g % BUFS], block_sem.at[g % BUFS])

    left = lax.broadcasted_iota(jnp.int32, (1, HALF), 1) < 64

    def beside(first, second):
        return jnp.where(left, first, second)

    def turn(value):
        return pltpu.roll(value, 64, 1)

    def solution_piece(c, u, k):
        if PACKED[c]:
            return x_pack.at[NARROW.index(c), u, pl.ds(k * 128, 128)]
        return x_wide.at[u, k]

    def band(c, i, high):
        if not PACKED[c]:
            return s_wide, (i, pl.ds(CUT, REST) if high else pl.ds(0, CUT))
        pair, k = PAIRS.index(UNITS[i][:2]), UNITS[i][2]
        rows = pl.ds(CUT + k * (REST // 2), REST // 2) if high else pl.ds(k * (CUT // 2), CUT // 2)
        return s_pack, (NARROW.index(c), pair, rows)

    def arrived(c, kind, *index):
        wide, pack = {"y": (y_wide, y_pack), "xy": (xy_wide, xy_pack), "x": (far_wide, far_pack), "last": (last_wide, last_pack)}[kind]
        return (pack, (NARROW.index(c), *index)) if PACKED[c] else (wide, index)

    def add(c, i, high, kind, *index):
        need((kind, c, *index))
        ref, at_rows = band(c, i, high)
        got, at_got = arrived(c, kind, *index)
        ref[at_rows] = ref[at_rows] + got[at_got]

    fetch_leaf = [
        pltpu.make_async_copy(src, dst, leaf_sem.at[i])
        for i, (src, dst) in enumerate(((leaf_inv_in, leaf_inv), (leaf_rhs_in, leaf_rhs)))
    ]
    for copy in fetch_leaf:
        copy.start()

    barrier = pltpu.get_barrier_semaphore()
    partners = (x_near, *z_to, other_core, x_far, *y_to)
    for partner in partners:
        pl.semaphore_signal(barrier, inc=1, device_id=partner, device_id_type=MESH)

    for g in range(BUFS):
        fetch(g).start()
    fetch_rhs = pltpu.make_async_copy(top_rhs, rhs, top_sem.at[0])
    fetch_inv = pltpu.make_async_copy(top_inv, inv, top_sem.at[1])
    fetch_rhs.start()
    fetch_inv.start()

    for k in range(CHAINS):
        chain[k, NONE] = jnp.zeros((W2, HALF), F32)

    for copy in fetch_leaf:
        copy.wait()

    started, seen = {}, set()

    def put(key):
        started[key] = message(*key)
        started[key].start()

    def need(*keys):
        for key in keys:
            if key not in seen:
                seen.add(key)
                message(*key).wait_recv()

    def message(kind, c, j, k=0):
        if kind == "near":
            ref = solution_piece(c, order[0] if j == 0 else order[4], k)
            return send(ref, ref, ax_s.at[c, j, k], ax_r.at[c, j, k], x_near)
        if kind == "z":
            u = (order[0], order[0], order[2 + j], order[1], order[1], order[5 + j])[k]
            ref = solution_piece(c, u, (j, 1 - j, j, 0, 1, j)[k])
            return send(ref, ref, az_s.at[c, j, k], az_r.at[c, j, k], z_to[j])
        if kind == "core":
            into = s_pack.at[NARROW.index(c), j] if PACKED[c] else s_wide.at[j]
            return send(give.at[j], into, core_s.at[c, j], core_r.at[c, j], other_core)
        if kind == "y":
            i, high, index, sems, device = Y_SEND[j][k], False, (j, k), (y_s, y_r), y_to[j]
        elif kind == "xy":
            i, high, index, sems, device = XY_SEND[j][k], True, (j, k), (xy_s, xy_r), y_to[j]
        elif kind == "x":
            i, high, index, sems, device = X_SEND[j], True, (j,), (x_s, x_r), x_far
        else:
            i, high, index, sems, device = 12 + j, False, (j,), (x2_s, x2_r), x_far
        src, at_src = band(c, i, high)
        dst, at_dst = arrived(c, kind, *index)
        return send(src.at[at_src], dst.at[at_dst], sems[0].at[(c, *index)], sems[1].at[(c, *index)], device)

    outs = []

    def out(src, dst, i):
        outs.append(pltpu.make_async_copy(src, dst, out_sem.at[i]))
        outs[-1].start()

    def solve(v, cols):
        i_high, i_low = split(leaf_inv[0, v])
        r_high, r_low = split(leaf_rhs[0, v, :, cols])
        solved = times(i_high, i_low, jnp.concatenate([r_high, r_low], axis=1), r_high)
        leaf_out[0, v, :, cols] = solved
        return solved

    def leaf(c):
        if PACKED[c]:
            first, second = solve(0, slice(0, HALF)), solve(1, slice(0, HALF))
            second = turn(second)
            x_pack[0, row] = beside(first, second)
            x_pack[1, row] = beside(second, first)
        else:
            for v in range(2):
                x_wide[row, v] = solve(v, slice(HALF, 2 * HALF))
            for v in range(2):
                out(leaf_out.at[0, v], leaf_to.at[0, v], v)

    def chains():
        lane = lax.broadcasted_iota(jnp.int32, (8, HALF), 1)
        ask, limit, slots = lane - 32, jnp.full((8, HALF), 32, jnp.int32), []
        for step in range(STEPS):
            for v in range(2):
                for a in range(2):
                    slot, b = step * 4 + v * 2 + a, a * 16 + order[step] * 2 + v
                    ask = jnp.where(lane == b, wanted[b], ask)
                    limit = jnp.where(lane == b, slot, limit)
                    slots.append((slot, wanted[b]))
        before = jnp.full((8, HALF), NONE, jnp.int32)
        for slot, its_row in slots:
            before = jnp.where((ask == its_row) & (limit > slot), slot, before)
        found[...] = before
        copy = pltpu.make_async_copy(found, meta, meta_sem.at[0])
        copy.start()
        copy.wait()

    def own(c):
        if c == 0:
            pl.semaphore_wait(barrier, len(partners))
        for j in range(2):
            put(("near", c, 0, j))
            for d in range(2):
                put(("z", c, d, j))

    def zpass(c, d):
        need(("z", c, d, 0))
        put(("z", c, d, 2))

    def near(c, j):
        need(("near", c, 0, j))
        for d in range(2):
            put(("z", c, d, 3 + j))

    def far(c, d):
        if FAR_BY_Z[c]:
            need(("z", c, d, 3 + d))
            put(("z", c, d, 5))
        else:
            need(("z", c, d, 2))
            put(("near", c, 1, d))

    def products(c, step):
        need(
            *(
                [],
                [("near", c, 0, 0), ("near", c, 0, 1)],
                [("z", c, 0, 0), ("z", c, 0, 1)],
                [("z", c, 1, 0), ("z", c, 1, 1)],
                [("z", c, 0, 2), ("z", c, 1, 2)],
                [("z", c, 0, 3), ("z", c, 0, 4)],
                [("z", c, 1, 3), ("z", c, 1, 4)],
                [("z", c, 0, 5), ("z", c, 1, 5)] if FAR_BY_Z[c] else [("near", c, 1, 0), ("near", c, 1, 1)],
            )[step]
        )
        g = c * STEPS + step
        u = order[step]
        fetch(g).wait()
        if PACKED[c]:
            k = NARROW.index(c)
            both = x_pack[k, u]
            turned = turn(both)
            columns = [beside(both, turned), beside(turned, both)]
            columns = columns if k == 0 else columns[::-1]
        else:
            columns = [x_wide[u, v] for v in range(2)]
        for v in range(2):
            high, low = split(columns[v])
            w[v, :, :HALF] = high
            w[v, :, HALF:] = low
        held = c % CHAINS

        def one(v, carry):
            for a in range(2):
                before = meta[0, a * 16 + u * 2 + v]
                for tile in range(2):
                    tall = slice(tile * 256, tile * 256 + 256)
                    b_high, b_low = split(blocks[g % BUFS, a, v, tall, :])
                    term = times(b_high, b_low, w[v], w[v, :, :HALF])
                    chain[held, step * 4 + v * 2 + a, tall, :] = term + chain[held, before, tall, :]
            return carry

        lax.fori_loop(0, 2, one, 0)
        if g + BUFS < PARTS * STEPS:
            fetch(g + BUFS).start()

    def total(c, i, its_core):
        dxh, dy = PAIRS[i] if PACKED[c] else UNITS[i][:2]
        first = ((xh + dxh) % 2) * 16 + ((y + dy) % 4) * 4 + its_core * 2
        if not PACKED[c]:
            return chain[c % CHAINS, meta[0, 32 + first + UNITS[i][2]]]
        pair = [chain[c % CHAINS, meta[0, 32 + first + e]] for e in range(2)]
        return beside(*(pair if NARROW.index(c) == 0 else pair[::-1]))

    def share_core(c, i):
        for before in range(c):
            if ("core", before, i) in started:
                started.pop(("core", before, i)).wait_send()
        give[i] = total(c, i, 1 - core)
        put(("core", c, i))

    def sum_core(c, i):
        need(("core", c, i))
        mine = total(c, i, core)
        if PACKED[c]:
            k = NARROW.index(c)
            s_pack[k, i] = s_pack[k, i] + mine
            units = [k for k in range(16) if UNITS[k][:2] == PAIRS[i]]
        else:
            s_wide[i] = s_wide[i] + mine
            units = [i]
        for unit in units:
            for d in range(2):
                if unit in Y_SEND[d][:4]:
                    put(("y", c, d, Y_SEND[d].index(unit)))
            if unit in X_SEND:
                put(("x", c, X_SEND.index(unit)))

    def y_add(c, i, js):
        for d in range(2):
            for j in js:
                if Y_ADD[d][j] == i:
                    add(c, i, False, "y", d, j)

    def pass_y(c, d, j):
        add(c, Y_ADD[d][j], False, "y", d, j)
        put(("y", c, d, 4 + j))

    def x_add(c, m):
        i = X_SEND[m] + 2
        add(c, i, True, "x", m)
        for d in range(2):
            if i in XY_SEND[d][:2]:
                put(("xy", c, d, XY_SEND[d].index(i)))

    def pass_xy(c, d):
        add(c, XY_ADD[d][0], True, "xy", d, 0)
        put(("xy", c, d, 2))

    def y_last(c, e):
        y_add(c, 12 + e, (2, 4))
        put(("last", c, e))

    def split_inv():
        fetch_rhs.wait()
        fetch_inv.wait()

        def one(i, carry):
            e, tall = i // 4, pl.ds(pl.multiple_of((i % 4) * 128, 128), 128)
            high, low = split(inv[e, tall, :])
            inv_high[e, tall, :] = high
            inv_low[e, tall, :] = low
            return carry

        lax.fori_loop(0, 8, one, 0)

    def finish(c, e):
        i = 14 + e
        y_add(c, i, (3, 5))
        for d in range(2):
            for j in (1, 2):
                if XY_ADD[d][j] == i:
                    add(c, i, True, "xy", d, j)
        add(c, i, False, "last", e)

    def top(wide, e):
        if wide:
            cols, update = slice(HALF, 2 * HALF), s_wide[14 + e]
        else:
            cols, pair = slice(0, HALF), PAIRS.index((0, 0))
            update = beside(*((s_pack[0, pair], s_pack[1, pair]) if e == 0 else (turn(s_pack[0, pair]), turn(s_pack[1, pair]))))
        high, low = split(rhs[e, :, cols] - update)
        both = jnp.concatenate([high, low], axis=1)
        top_out[e, :256, cols] = times(inv_high[e, :256, :256], inv_low[e, :256, :256], both[:256], high[:256])
        top_out[e, 256:, cols] = times(inv_high[e, 256:], inv_low[e, 256:], both, high)
        out(top_out.at[e, :, cols], top_to.at[e, :, cols], 2 + wide * 2 + e)

    tasks = {
        "leaf": leaf, "own": own, "zpass": zpass, "near": near, "far": far, "p": products, "inv": split_inv,
        "give": share_core, "sum": sum_core, "ypass": pass_y, "xadd": x_add, "xypass": pass_xy,
        "ylast": y_last, "fin": finish, "top": top, "chains": chains,
    }
    for name, *numbers in ORDER:
        tasks[name](*numbers)
    for copy in started.values():
        copy.wait_send()
    for copy in outs:
        copy.wait()


def hand_over(leaf_in, top_in, leaf_out, top_out, leaf, top, sem):
    pieces = [(ref.at[0, v], held.at[0, v], out.at[0, v]) for ref, held, out in ((leaf_in, leaf, leaf_out),) for v in range(2)]
    pieces += [
        (top_in.at[e, half], top.at[e, half], top_out.at[e, half])
        for e in range(2)
        for half in (pl.ds(0, 256), pl.ds(256, 256))
    ]
    loads = [pltpu.make_async_copy(src, held, sem.at[0, i]) for i, (src, held, _) in enumerate(pieces)]
    stores = [pltpu.make_async_copy(held, out, sem.at[1, i]) for i, (_, held, out) in enumerate(pieces)]
    for load in loads:
        load.start()
    for load, store in zip(loads, stores):
        load.wait()
        store.start()
    for store in stores:
        store.wait()


def per_device(leaf_rhs, leaf_inverse, off_blocks, ancestor_rows, block_present, top_rhs, top_inverse):
    wanted = jnp.where(block_present != 0, ancestor_rows, -1).reshape(-1)
    smem = pl.BlockSpec(memory_space=pltpu.SMEM)
    anywhere = pl.BlockSpec(memory_space=pl.ANY)
    dma = pltpu.SemaphoreType.DMA
    leaf, top = pl.pallas_call(
        kernel,
        out_shape=(
            jax.ShapeDtypeStruct(leaf_rhs.shape, F32),
            jax.ShapeDtypeStruct(top_rhs.shape, F32),
        ),
        in_specs=[smem] + [anywhere] * 5,
        out_specs=(anywhere, anywhere),
        scratch_shapes=[
            pltpu.VMEM(leaf_rhs.shape, F32),
            pltpu.VMEM(leaf_inverse.shape, F32),
            pltpu.VMEM(leaf_rhs.shape, F32),
            pltpu.VMEM(top_rhs.shape, F32),
            pltpu.VMEM((8, HALF), jnp.int32),
            pltpu.SMEM((8, HALF), jnp.int32),
            pltpu.VMEM((8, 2, W1, HALF), F32),
            pltpu.VMEM((2, 8, W1, HALF), F32),
            pltpu.VMEM((2, W1, 2 * HALF), BF16),
            pltpu.VMEM((BUFS, 2, 2, W2, W1), F32),
            pltpu.VMEM((CHAINS, NONE + 1, W2, HALF), F32),
            pltpu.VMEM((16, W2, HALF), F32),
            pltpu.VMEM((16, W2, HALF), F32),
            pltpu.VMEM((2, 8, W2, HALF), F32),
            pltpu.VMEM((2, 6, CUT, HALF), F32),
            pltpu.VMEM((2, 2, 6, CUT // 2, HALF), F32),
            pltpu.VMEM((2, 3, REST, HALF), F32),
            pltpu.VMEM((2, 2, 3, REST // 2, HALF), F32),
            pltpu.VMEM((8, REST, HALF), F32),
            pltpu.VMEM((2, 8, REST // 2, HALF), F32),
            pltpu.VMEM((2, CUT, HALF), F32),
            pltpu.VMEM((2, 2, CUT // 2, HALF), F32),
            pltpu.VMEM((2, W2, 2 * HALF), F32),
            pltpu.VMEM((2, W2, W2), F32),
            pltpu.VMEM((2, W2, W2), BF16),
            pltpu.VMEM((2, W2, W2), BF16),
            dma((BUFS,)),
            dma((2,)),
            dma((2,)),
            dma((6,)),
            dma((1,)),
            *(dma((PARTS, *shape)) for shape in ((2, 6), (2, 2), (16,), (2, 6), (2, 3), (8,), (2,)) for _ in range(2)),
        ],
        compiler_params=pltpu.CompilerParams(
            collective_id=0, has_side_effects=True, vmem_limit_bytes=60 * 1024 * 1024
        ),
        cost_estimate=pl.CostEstimate(flops=7_500_000_000, bytes_accessed=40_000_000, transcendentals=0),
    )(wanted, leaf_rhs, leaf_inverse, off_blocks, top_rhs, top_inverse)
    return pl.pallas_call(
        hand_over,
        out_shape=(jax.ShapeDtypeStruct(leaf_rhs.shape, F32), jax.ShapeDtypeStruct(top_rhs.shape, F32)),
        in_specs=[anywhere, anywhere],
        out_specs=(anywhere, anywhere),
        scratch_shapes=[pltpu.VMEM(leaf_rhs.shape, F32), pltpu.VMEM(top_rhs.shape, F32), dma((2, 6))],
    )(leaf, top)


def solution(mesh):
    return jax.shard_map(
        per_device,
        mesh=mesh,
        in_specs=(
            P("prow", "pcol", None, None),
            P("prow", "pcol", None, None),
            P("prow", None, None, "pcol", None, None),
            P("prow", None, None, "pcol"),
            P("prow", None, None, "pcol"),
            P(("prow", "pcol"), None, None),
            P(("prow", "pcol"), None, None),
        ),
        out_specs=(P("prow", "pcol", None, None), P(("prow", "pcol"), None, None)),
        check_vma=False,
    )
```

```python
import jax
import jax.numpy as jnp
from jax import lax
from jax.experimental import pallas as pl
from jax.experimental.pallas import tpu as pltpu
from jax.sharding import PartitionSpec as P

MESH = pl.DeviceIdType.MESH
F32, BF16 = jnp.float32, jnp.bfloat16
W1, W2, HALF = 256, 512, 128
STEPS = 8
BUFS = 3
CUT, REST = 296, 216
CUT_PACKED, REST_PACKED = 144, 112
NONE = 32
PACKED = (True, True, False)
PARTS = len(PACKED)
NARROW = tuple(c for c in range(PARTS) if PACKED[c])
CHAINS = 2
X_ONLY, BOTH, Z_ONLY = 0, 2, 1
FAR_BY = (2, 1, 1)

UNITS = (
    (1, 2, 0), (1, 2, 1), (0, 2, 0), (0, 2, 1),
    (1, 1, 1), (1, 3, 0), (0, 1, 1), (0, 3, 0),
    (1, 1, 0), (1, 3, 1), (0, 1, 0), (0, 3, 1),
    (1, 0, 0), (1, 0, 1), (0, 0, 0), (0, 0, 1),
)
PAIRS = ((1, 2), (0, 2), (1, 1), (1, 3), (0, 1), (0, 3), (1, 0), (0, 0))
Y_SEND = ((0, 2, 4, 6, 8, 10), (1, 3, 5, 7, 9, 11))
Y_ADD = ((8, 10, 13, 15, 12, 14), (9, 11, 12, 14, 13, 15))
X_SEND = (0, 1, 4, 5, 8, 9, 12, 13)
XY_SEND = ((2, 6, 10), (3, 7, 11))
XY_ADD = ((10, 15, 14), (11, 14, 15))


ORDER = (
    ("leaf", 0), ("ownx", 0, 1), ("ownz", 0), ("ownx", 0, 0), ("chains",), ("p", 0, 0), ("leaf", 2), ("ownx", 1, 1),
    ("ownx", 1, 0), ("inv",), ("near", 0, 1), ("zpass", 0, 0), ("zpass", 0, 1), ("near", 0, 0), ("p", 0, 1),
    ("p", 0, 2), ("p", 0, 3), ("far", 0, 1), ("far", 0, 0), ("ownz", 1), ("near", 1, 1), ("p", 0, 4), ("near", 1, 0),
    ("ownx", 2, 1), ("ownx", 2, 0), ("p", 0, 5), ("p", 0, 6), ("p", 0, 7), ("give", 0, 0), ("zpass", 1, 0),
    ("give", 0, 1), ("p", 1, 0), ("p", 1, 1), ("give", 0, 2), ("zpass", 1, 1), ("give", 0, 3), ("give", 0, 4),
    ("give", 0, 5), ("far", 1, 1), ("sum", 0, 0), ("give", 0, 6), ("give", 0, 7), ("p", 1, 2), ("far", 1, 0),
    ("sum", 0, 1), ("ownz", 2), ("near", 2, 1), ("p", 1, 3), ("near", 2, 0), ("sum", 0, 2), ("sum", 0, 3),
    ("p", 1, 4), ("sum", 0, 4), ("ypass", 0, 1, 0), ("sum", 0, 5), ("xadd", 0, 0), ("sum", 0, 6), ("xadd", 0, 1),
    ("sum", 0, 7), ("ypass", 0, 0, 0), ("p", 1, 5), ("ypass", 0, 1, 1), ("ypass", 0, 0, 1), ("p", 1, 6),
    ("zpass", 2, 1), ("xadd", 0, 2), ("p", 1, 7), ("give", 1, 0), ("give", 1, 1), ("give", 1, 2), ("ylast", 0, 1),
    ("xadd", 0, 3), ("xadd", 0, 4), ("zpass", 2, 0), ("p", 2, 0), ("xadd", 0, 5), ("give", 1, 3), ("give", 1, 4),
    ("give", 1, 5), ("give", 1, 6), ("give", 1, 7), ("p", 2, 1), ("sum", 1, 0), ("xypass", 0, 1), ("sum", 1, 1),
    ("xadd", 0, 6), ("sum", 1, 2), ("ylast", 0, 0), ("xadd", 0, 7), ("xypass", 0, 0), ("p", 2, 2), ("far", 2, 1),
    ("p", 2, 3), ("finy", 0, 1), ("sum", 1, 3), ("sum", 1, 4), ("sum", 1, 5), ("sum", 1, 6), ("sum", 1, 7),
    ("xadd", 1, 0), ("ypass", 1, 1, 0), ("ypass", 1, 0, 0), ("far", 2, 0), ("xadd", 1, 1), ("finx", 0, 1),
    ("ypass", 1, 0, 1), ("xadd", 1, 2), ("ypass", 1, 1, 1), ("p", 2, 4), ("p", 2, 5), ("xadd", 1, 4), ("finx", 0, 0),
    ("p", 2, 6), ("p", 2, 7), ("xypass", 1, 0), ("give", 2, 0), ("xadd", 1, 3), ("xadd", 1, 5), ("ylast", 1, 1),
    ("finy", 0, 0), ("give", 2, 1), ("give", 2, 2), ("give", 2, 3), ("give", 2, 4), ("give", 2, 5), ("xadd", 1, 6),
    ("give", 2, 6), ("give", 2, 7), ("ylast", 1, 0), ("xypass", 1, 1), ("give", 2, 8), ("give", 2, 9),
    ("give", 2, 10), ("give", 2, 11), ("give", 2, 12), ("give", 2, 13), ("xadd", 1, 7), ("give", 2, 14),
    ("give", 2, 15), ("sum", 2, 0), ("sum", 2, 1), ("sum", 2, 2), ("finy", 1, 1), ("sum", 2, 3), ("sum", 2, 4),
    ("sum", 2, 5), ("finx", 1, 1), ("finx", 1, 0), ("finy", 1, 0), ("top", 1), ("top", 0), ("sum", 2, 6),
    ("sum", 2, 7), ("sum", 2, 8), ("sum", 2, 9), ("xadd", 2, 0), ("sum", 2, 10), ("sum", 2, 11), ("ypass", 2, 0, 0),
    ("ypass", 2, 1, 0), ("sum", 2, 12), ("sum", 2, 13), ("sum", 2, 14), ("xadd", 2, 1), ("sum", 2, 15),
    ("ypass", 2, 0, 1), ("ypass", 2, 1, 1), ("xadd", 2, 2), ("xadd", 2, 3), ("xadd", 2, 4), ("xadd", 2, 5),
    ("xypass", 2, 0), ("ylast", 2, 1), ("xadd", 2, 6), ("ylast", 2, 0), ("xypass", 2, 1), ("xadd", 2, 7),
    ("finy", 2, 1), ("topa", 1), ("finy", 2, 0), ("topa", 0), ("finx", 2, 0), ("topb", 0), ("finx", 2, 1),
    ("topb", 1),
)

def split(value):
    high = value.astype(BF16)
    return high, (value - high.astype(F32)).astype(BF16)


def dot(a, b):
    return jnp.dot(a, b, preferred_element_type=F32)


def times(a_high, a_low, both, high):
    wide = dot(a_high, both)
    return wide[:, :HALF] + wide[:, HALF:] + dot(a_low, high)


def kernel(
    wanted_in, leaf_rhs_in, leaf_inv_in, off_blocks, top_rhs, top_inv, leaf_to, top_to,
    leaf_rhs, leaf_inv, leaf_out, top_out, wanted, found, meta,
    x_wide, x_pack, w, blocks, chain, give, s_wide, s_pack, y_wide, y_pack, xy_wide, xy_pack, far_wide, far_pack,
    last_wide, last_pack, rhs, inv, inv_high, inv_low,
    block_sem, top_sem, leaf_sem, out_sem, meta_sem, az_s, az_r, ax_s, ax_r, core_s, core_r, y_s, y_r, xy_s, xy_r, x_s, x_r, x2_s, x2_r,
):
    row, col = lax.axis_index("prow"), lax.axis_index("pcol")
    z, xl = row // 2, row % 2
    xh, y, core = col // 8, (col // 2) % 4, col % 2

    def rows_at(dz, dx):
        return ((z + dz) % 4) * 2 + (xl + dx) % 2

    def at(dxh, dy, dcore):
        return ((xh + dxh) % 2) * 8 + ((y + dy) % 4) * 2 + (core + dcore) % 2

    x_near = (rows_at(0, 1), col)
    z_to = ((rows_at(1, 0), col), (rows_at(3, 0), col))
    other_core = (row, at(0, 0, 1))
    x_far = (row, at(1, 0, 0))
    y_to = ((row, at(0, 1, 0)), (row, at(0, 3, 0)))
    order = [rows_at(*d) for d in ((0, 0), (0, 1), (3, 0), (1, 0), (2, 0), (3, 1), (1, 1), (2, 1))]

    def send(src, dst, send_sem, recv_sem, device):
        return pltpu.make_async_remote_copy(
            src_ref=src, dst_ref=dst, send_sem=send_sem, recv_sem=recv_sem, device_id=device, device_id_type=MESH
        )

    def fetch(g):
        u = order[g % STEPS]
        return pltpu.make_async_copy(off_blocks.at[0, :, u], blocks.at[g % BUFS], block_sem.at[g % BUFS])

    left = lax.broadcasted_iota(jnp.int32, (1, HALF), 1) < 64

    def beside(first, second):
        return jnp.where(left, first, second)

    def turn(value):
        return pltpu.roll(value, 64, 1)

    def solution_piece(c, u, k):
        if PACKED[c]:
            return x_pack.at[NARROW.index(c), u, pl.ds(k * 128, 128)]
        return x_wide.at[u, k]

    def band(c, i, high):
        if not PACKED[c]:
            return s_wide, (i, pl.ds(CUT, REST) if high else pl.ds(0, CUT))
        pair, k = PAIRS.index(UNITS[i][:2]), UNITS[i][2]
        rows = pl.ds(2 * CUT_PACKED + k * REST_PACKED, REST_PACKED) if high else pl.ds(k * CUT_PACKED, CUT_PACKED)
        return s_pack, (NARROW.index(c), pair, rows)

    def arrived(c, kind, *index):
        wide, pack = {"y": (y_wide, y_pack), "xy": (xy_wide, xy_pack), "x": (far_wide, far_pack), "last": (last_wide, last_pack)}[kind]
        return (pack, (NARROW.index(c), *index)) if PACKED[c] else (wide, index)

    def add(c, i, high, kind, *index):
        need((kind, c, *index))
        ref, at_rows = band(c, i, high)
        got, at_got = arrived(c, kind, *index)
        ref[at_rows] = ref[at_rows] + got[at_got]

    fetch_leaf = [
        pltpu.make_async_copy(src, dst, leaf_sem.at[i])
        for i, (src, dst) in enumerate(((leaf_inv_in, leaf_inv), (leaf_rhs_in, leaf_rhs)))
    ]
    fetch_wanted = pltpu.make_async_copy(wanted_in, wanted, meta_sem.at[1])
    for copy in (*fetch_leaf, fetch_wanted):
        copy.start()

    barrier = pltpu.get_barrier_semaphore()
    partners = (x_near, *z_to, other_core, x_far, *y_to)
    for partner in partners:
        pl.semaphore_signal(barrier, inc=1, device_id=partner, device_id_type=MESH)

    for g in range(BUFS):
        fetch(g).start()
    fetch_rhs = pltpu.make_async_copy(top_rhs, rhs, top_sem.at[0])
    fetch_inv = pltpu.make_async_copy(top_inv, inv, top_sem.at[1])
    fetch_rhs.start()
    fetch_inv.start()

    for k in range(CHAINS):
        chain[k, NONE] = jnp.zeros((W2, HALF), F32)

    for copy in fetch_leaf:
        copy.wait()

    started, seen = {}, set()

    def put(key):
        if not started:
            pl.semaphore_wait(barrier, len(partners))
        started[key] = message(*key)
        started[key].start()

    def need(*keys):
        for key in keys:
            if key not in seen:
                seen.add(key)
                message(*key).wait_recv()

    def message(kind, c, j, k=0):
        if kind == "near":
            ref = solution_piece(c, order[0] if j == 0 else order[4], k)
            return send(ref, ref, ax_s.at[c, j, k], ax_r.at[c, j, k], x_near)
        if kind == "z":
            u = (order[0], order[0], order[2 + j], order[1], order[1], order[5 + j])[k]
            ref = solution_piece(c, u, (j, 1 - j, j, 0, 1, j)[k])
            return send(ref, ref, az_s.at[c, j, k], az_r.at[c, j, k], z_to[j])
        if kind == "core":
            into = s_pack.at[NARROW.index(c), j] if PACKED[c] else s_wide.at[j]
            return send(give.at[j], into, core_s.at[c, j], core_r.at[c, j], other_core)
        if kind == "y":
            i, high, index, sems, device = Y_SEND[j][k], False, (j, k), (y_s, y_r), y_to[j]
        elif kind == "xy":
            i, high, index, sems, device = XY_SEND[j][k], True, (j, k), (xy_s, xy_r), y_to[j]
        elif kind == "x":
            i, high, index, sems, device = X_SEND[j], True, (j,), (x_s, x_r), x_far
        else:
            i, high, index, sems, device = 12 + j, False, (j,), (x2_s, x2_r), x_far
        src, at_src = band(c, i, high)
        dst, at_dst = arrived(c, kind, *index)
        return send(src.at[at_src], dst.at[at_dst], sems[0].at[(c, *index)], sems[1].at[(c, *index)], device)

    outs = []

    def out(src, dst, i):
        outs.append(pltpu.make_async_copy(src, dst, out_sem.at[i]))
        outs[-1].start()

    def solve(v, cols):
        i_high, i_low = split(leaf_inv[0, v])
        r_high, r_low = split(leaf_rhs[0, v, :, cols])
        solved = times(i_high, i_low, jnp.concatenate([r_high, r_low], axis=1), r_high)
        leaf_out[0, v, :, cols] = solved
        return solved

    def leaf(c):
        if PACKED[c]:
            first, second = solve(0, slice(0, HALF)), solve(1, slice(0, HALF))
            second = turn(second)
            x_pack[0, row] = beside(first, second)
            x_pack[1, row] = beside(second, first)
        else:
            for v in range(2):
                x_wide[row, v] = solve(v, slice(HALF, 2 * HALF))
            for v in range(2):
                out(leaf_out.at[0, v], leaf_to.at[0, v], v)

    def chains():
        fetch_wanted.wait()
        lane = lax.broadcasted_iota(jnp.int32, (8, HALF), 1)
        ask, limit, slots = lane - 32, jnp.full((8, HALF), 32, jnp.int32), []
        for step in range(STEPS):
            for v in range(2):
                for a in range(2):
                    slot, b = step * 4 + v * 2 + a, a * 16 + order[step] * 2 + v
                    ask = jnp.where(lane == b, wanted[b], ask)
                    limit = jnp.where(lane == b, slot, limit)
                    slots.append((slot, wanted[b]))
        before = jnp.full((8, HALF), NONE, jnp.int32)
        for slot, its_row in slots:
            before = jnp.where((ask == its_row) & (limit > slot), slot, before)
        found[...] = before
        copy = pltpu.make_async_copy(found, meta, meta_sem.at[0])
        copy.start()
        copy.wait()

    def own_x(c, v):
        put(("near", c, 0, v))

    def own_z(c):
        for j in range(2):
            for d in range(2):
                put(("z", c, d, j))

    def zpass(c, d):
        need(("z", c, d, 0))
        put(("z", c, d, 2))

    def near(c, j):
        need(("near", c, 0, j))
        for d in range(2):
            put(("z", c, d, 3 + j))

    def far(c, d):
        if FAR_BY[c] == Z_ONLY or (FAR_BY[c] == BOTH and d == 1):
            need(("z", c, d, 3 + d))
            put(("z", c, d, 5))
        else:
            need(("z", c, d, 2))
            put(("near", c, 1, d))

    def products(c, step):
        need(
            *(
                [],
                [("near", c, 0, 0), ("near", c, 0, 1)],
                [("z", c, 0, 0), ("z", c, 0, 1)],
                [("z", c, 1, 0), ("z", c, 1, 1)],
                [("z", c, 0, 2), ("z", c, 1, 2)],
                [("z", c, 0, 3), ("z", c, 0, 4)],
                [("z", c, 1, 3), ("z", c, 1, 4)],
                [
                    ("near", c, 1, d) if FAR_BY[c] == X_ONLY or (FAR_BY[c] == BOTH and d == 0) else ("z", c, d, 5)
                    for d in range(2)
                ],
            )[step]
        )
        g = c * STEPS + step
        u = order[step]
        fetch(g).wait()
        if PACKED[c]:
            k = NARROW.index(c)
            both = x_pack[k, u]
            turned = turn(both)
            columns = [beside(both, turned), beside(turned, both)]
            columns = columns if k == 0 else columns[::-1]
        else:
            columns = [x_wide[u, v] for v in range(2)]
        for v in range(2):
            high, low = split(columns[v])
            w[v, :, :HALF] = high
            w[v, :, HALF:] = low
        held = c % CHAINS

        def one(v, carry=0):
            for a in range(2):
                before = meta[0, a * 16 + u * 2 + v]
                for tile in range(2):
                    tall = slice(tile * 256, tile * 256 + 256)
                    b_high, b_low = split(blocks[g % BUFS, a, v, tall, :])
                    term = times(b_high, b_low, w[v], w[v, :, :HALF])
                    chain[held, step * 4 + v * 2 + a, tall, :] = term + chain[held, before, tall, :]
            return carry

        if c == 0:
            one(0), one(1)
        else:
            lax.fori_loop(0, 2, one, 0)
        if g + BUFS < PARTS * STEPS:
            fetch(g + BUFS).start()

    def total(c, i, its_core):
        dxh, dy = PAIRS[i] if PACKED[c] else UNITS[i][:2]
        first = ((xh + dxh) % 2) * 16 + ((y + dy) % 4) * 4 + its_core * 2
        if not PACKED[c]:
            return chain[c % CHAINS, meta[0, 32 + first + UNITS[i][2]]]
        pair = [chain[c % CHAINS, meta[0, 32 + first + e]] for e in range(2)]
        return beside(*(pair if NARROW.index(c) == 0 else pair[::-1]))

    def share_core(c, i):
        for before in range(c):
            if ("core", before, i) in started:
                started.pop(("core", before, i)).wait_send()
        give[i] = total(c, i, 1 - core)
        put(("core", c, i))

    def sum_core(c, i):
        need(("core", c, i))
        mine = total(c, i, core)
        if PACKED[c]:
            k = NARROW.index(c)
            s_pack[k, i] = s_pack[k, i] + mine
            units = [k for k in range(16) if UNITS[k][:2] == PAIRS[i]]
        else:
            s_wide[i] = s_wide[i] + mine
            units = [i]
        for unit in units:
            for d in range(2):
                if unit in Y_SEND[d][:4]:
                    put(("y", c, d, Y_SEND[d].index(unit)))
            if unit in X_SEND:
                put(("x", c, X_SEND.index(unit)))

    def y_add(c, i, js):
        for d in range(2):
            for j in js:
                if Y_ADD[d][j] == i:
                    add(c, i, False, "y", d, j)

    def pass_y(c, d, j):
        add(c, Y_ADD[d][j], False, "y", d, j)
        put(("y", c, d, 4 + j))

    def x_add(c, m):
        i = X_SEND[m] + 2
        add(c, i, True, "x", m)
        for d in range(2):
            if i in XY_SEND[d][:2]:
                put(("xy", c, d, XY_SEND[d].index(i)))

    def pass_xy(c, d):
        add(c, XY_ADD[d][0], True, "xy", d, 0)
        put(("xy", c, d, 2))

    def y_last(c, e):
        y_add(c, 12 + e, (2, 4))
        put(("last", c, e))

    def split_inv():
        fetch_rhs.wait()
        fetch_inv.wait()

        def one(i, carry):
            e, tall = i // 4, pl.ds(pl.multiple_of((i % 4) * 128, 128), 128)
            high, low = split(inv[e, tall, :])
            inv_high[e, tall, :] = high
            inv_low[e, tall, :] = low
            return carry

        lax.fori_loop(0, 8, one, 0)

    def finish_y(c, e):
        y_add(c, 14 + e, (3, 5))
        add(c, 14 + e, False, "last", e)

    def finish_xy(c, e):
        for d in range(2):
            for j in (1, 2):
                if XY_ADD[d][j] == 14 + e:
                    add(c, 14 + e, True, "xy", d, j)

    def block_times(e, below, right, value):
        high, low = split(value)
        both = jnp.concatenate([high, low], axis=1)
        return times(inv_high[e, below, right], inv_low[e, below, right], both, high)

    upper, lower, whole = slice(0, 256), slice(256, W2), slice(0, W2)
    narrow_cols, wide_cols = slice(0, HALF), slice(HALF, 2 * HALF)

    def top(e):
        pair = PAIRS.index((0, 0))
        sums = [s_pack[k, pair] for k in range(2)]
        value = rhs[e, :, narrow_cols] - (beside(*sums) if e == 0 else beside(*map(turn, sums)))
        top_out[e, upper, narrow_cols] = block_times(e, upper, upper, value[:256])
        top_out[e, lower, narrow_cols] = block_times(e, lower, whole, value)
        out(top_out.at[e, :, narrow_cols], top_to.at[e, :, narrow_cols], 2 + e)

    def top_upper(e):
        value = rhs[e, upper, wide_cols] - s_wide[14 + e, upper]
        top_out[e, upper, wide_cols] = block_times(e, upper, upper, value)
        top_out[e, lower, wide_cols] = block_times(e, lower, upper, value)
        out(top_out.at[e, upper, wide_cols], top_to.at[e, upper, wide_cols], 4 + e)

    def top_lower(e):
        value = rhs[e, lower, wide_cols] - s_wide[14 + e, lower]
        top_out[e, lower, wide_cols] = top_out[e, lower, wide_cols] + block_times(e, lower, lower, value)
        out(top_out.at[e, lower, wide_cols], top_to.at[e, lower, wide_cols], 6 + e)

    tasks = {
        "leaf": leaf, "ownx": own_x, "ownz": own_z, "zpass": zpass, "near": near, "far": far, "p": products, "inv": split_inv,
        "give": share_core, "sum": sum_core, "ypass": pass_y, "xadd": x_add, "xypass": pass_xy,
        "ylast": y_last, "finy": finish_y, "finx": finish_xy, "top": top, "topa": top_upper, "topb": top_lower,
        "chains": chains,
    }
    for name, *numbers in ORDER:
        tasks[name](*numbers)
    for copy in started.values():
        copy.wait_send()
    for copy in outs:
        copy.wait()


def hand_over(leaf_in, top_in, leaf_out, top_out, leaf, top, sem):
    pieces = [(ref.at[0, v], held.at[0, v], out.at[0, v]) for ref, held, out in ((leaf_in, leaf, leaf_out),) for v in range(2)]
    pieces += [
        (top_in.at[e, half], top.at[e, half], top_out.at[e, half])
        for e in range(2)
        for half in (pl.ds(0, 256), pl.ds(256, 256))
    ]
    loads = [pltpu.make_async_copy(src, held, sem.at[0, i]) for i, (src, held, _) in enumerate(pieces)]
    stores = [pltpu.make_async_copy(held, out, sem.at[1, i]) for i, (_, held, out) in enumerate(pieces)]
    for load in loads:
        load.start()
    for load, store in zip(loads, stores):
        load.wait()
        store.start()
    for store in stores:
        store.wait()


def per_device(leaf_rhs, leaf_inverse, off_blocks, ancestor_rows, block_present, top_rhs, top_inverse):
    wanted = jnp.where(block_present != 0, ancestor_rows, -1).reshape(-1)
    anywhere = pl.BlockSpec(memory_space=pl.ANY)
    dma = pltpu.SemaphoreType.DMA
    leaf, top = pl.pallas_call(
        kernel,
        out_shape=(
            jax.ShapeDtypeStruct(leaf_rhs.shape, F32),
            jax.ShapeDtypeStruct(top_rhs.shape, F32),
        ),
        in_specs=[anywhere] * 6,
        out_specs=(anywhere, anywhere),
        scratch_shapes=[
            pltpu.VMEM(leaf_rhs.shape, F32),
            pltpu.VMEM(leaf_inverse.shape, F32),
            pltpu.VMEM(leaf_rhs.shape, F32),
            pltpu.VMEM(top_rhs.shape, F32),
            pltpu.SMEM((32,), jnp.int32),
            pltpu.VMEM((8, HALF), jnp.int32),
            pltpu.SMEM((8, HALF), jnp.int32),
            pltpu.VMEM((8, 2, W1, HALF), F32),
            pltpu.VMEM((2, 8, W1, HALF), F32),
            pltpu.VMEM((2, W1, 2 * HALF), BF16),
            pltpu.VMEM((BUFS, 2, 2, W2, W1), F32),
            pltpu.VMEM((CHAINS, NONE + 1, W2, HALF), F32),
            pltpu.VMEM((16, W2, HALF), F32),
            pltpu.VMEM((16, W2, HALF), F32),
            pltpu.VMEM((2, 8, W2, HALF), F32),
            pltpu.VMEM((2, 6, CUT, HALF), F32),
            pltpu.VMEM((2, 2, 6, CUT_PACKED, HALF), F32),
            pltpu.VMEM((2, 3, REST, HALF), F32),
            pltpu.VMEM((2, 2, 3, REST_PACKED, HALF), F32),
            pltpu.VMEM((8, REST, HALF), F32),
            pltpu.VMEM((2, 8, REST_PACKED, HALF), F32),
            pltpu.VMEM((2, CUT, HALF), F32),
            pltpu.VMEM((2, 2, CUT_PACKED, HALF), F32),
            pltpu.VMEM((2, W2, 2 * HALF), F32),
            pltpu.VMEM((2, W2, W2), F32),
            pltpu.VMEM((2, W2, W2), BF16),
            pltpu.VMEM((2, W2, W2), BF16),
            dma((BUFS,)),
            dma((2,)),
            dma((2,)),
            dma((8,)),
            dma((2,)),
            *(dma((PARTS, *shape)) for shape in ((2, 6), (2, 2), (16,), (2, 6), (2, 3), (8,), (2,)) for _ in range(2)),
        ],
        compiler_params=pltpu.CompilerParams(
            collective_id=0, has_side_effects=True, vmem_limit_bytes=60 * 1024 * 1024
        ),
        cost_estimate=pl.CostEstimate(flops=7_500_000_000, bytes_accessed=40_000_000, transcendentals=0),
    )(wanted, leaf_rhs, leaf_inverse, off_blocks, top_rhs, top_inverse)
    return pl.pallas_call(
        hand_over,
        out_shape=(jax.ShapeDtypeStruct(leaf_rhs.shape, F32), jax.ShapeDtypeStruct(top_rhs.shape, F32)),
        in_specs=[anywhere, anywhere],
        out_specs=(anywhere, anywhere),
        scratch_shapes=[pltpu.VMEM(leaf_rhs.shape, F32), pltpu.VMEM(top_rhs.shape, F32), dma((2, 6))],
    )(leaf, top)


def solution(mesh):
    return jax.shard_map(
        per_device,
        mesh=mesh,
        in_specs=(
            P("prow", "pcol", None, None),
            P("prow", "pcol", None, None),
            P("prow", None, None, "pcol", None, None),
            P("prow", None, None, "pcol"),
            P("prow", None, None, "pcol"),
            P(("prow", "pcol"), None, None),
            P(("prow", "pcol"), None, None),
        ),
        out_specs=(P("prow", "pcol", None, None), P(("prow", "pcol"), None, None)),
        check_vma=False,
    )
```

```python
import jax
import jax.numpy as jnp
from jax import lax
from jax.experimental import pallas as pl
from jax.experimental.pallas import tpu as pltpu
from jax.sharding import PartitionSpec as P

MESH = pl.DeviceIdType.MESH
F32, BF16 = jnp.float32, jnp.bfloat16
W1, W2, HALF = 256, 512, 128
STEPS = 8
BUFS = 3
CUT, REST = 296, 216
CUT_PACKED, REST_PACKED = 144, 112
NONE = 32
PACKED = (True, True, False)
PARTS = len(PACKED)
NARROW = tuple(c for c in range(PARTS) if PACKED[c])
CHAINS = 2
X_ONLY, BOTH, Z_ONLY = 0, 2, 1
FAR_BY = (2, 1, 1)

UNITS = (
    (1, 2, 0), (1, 2, 1), (0, 2, 0), (0, 2, 1),
    (1, 1, 1), (1, 3, 0), (0, 1, 1), (0, 3, 0),
    (1, 1, 0), (1, 3, 1), (0, 1, 0), (0, 3, 1),
    (1, 0, 0), (1, 0, 1), (0, 0, 0), (0, 0, 1),
)
PAIRS = ((1, 2), (0, 2), (1, 1), (1, 3), (0, 1), (0, 3), (1, 0), (0, 0))
Y_SEND = ((0, 2, 4, 6, 8, 10), (1, 3, 5, 7, 9, 11))
Y_ADD = ((8, 10, 13, 15, 12, 14), (9, 11, 12, 14, 13, 15))
X_SEND = (0, 1, 4, 5, 8, 9, 12, 13)
XY_SEND = ((2, 6, 10), (3, 7, 11))
XY_ADD = ((10, 15, 14), (11, 14, 15))


ORDER = (
    ("leaf", 0), ("ownx", 0, 1), ("ownz", 0), ("ownx", 0, 0), ("chains",), ("p", 0, 0), ("leaf", 2), ("ownx", 1, 1),
    ("ownx", 1, 0), ("inv",), ("near", 0, 1), ("zpass", 0, 0), ("zpass", 0, 1), ("near", 0, 0), ("p", 0, 1),
    ("p", 0, 2), ("p", 0, 3), ("far", 0, 1), ("far", 0, 0), ("ownz", 1), ("near", 1, 1), ("p", 0, 4), ("near", 1, 0),
    ("ownx", 2, 1), ("ownx", 2, 0), ("p", 0, 5), ("p", 0, 6), ("p", 0, 7), ("give", 0, 0), ("zpass", 1, 0),
    ("give", 0, 1), ("p", 1, 0), ("p", 1, 1), ("give", 0, 2), ("zpass", 1, 1), ("give", 0, 3), ("give", 0, 4),
    ("give", 0, 5), ("far", 1, 1), ("sum", 0, 0), ("give", 0, 6), ("give", 0, 7), ("p", 1, 2), ("far", 1, 0),
    ("sum", 0, 1), ("ownz", 2), ("near", 2, 1), ("p", 1, 3), ("near", 2, 0), ("sum", 0, 2), ("sum", 0, 3),
    ("p", 1, 4), ("sum", 0, 4), ("ypass", 0, 1, 0), ("sum", 0, 5), ("xadd", 0, 0), ("sum", 0, 6), ("xadd", 0, 1),
    ("sum", 0, 7), ("ypass", 0, 0, 0), ("p", 1, 5), ("ypass", 0, 1, 1), ("ypass", 0, 0, 1), ("p", 1, 6),
    ("zpass", 2, 1), ("xadd", 0, 2), ("p", 1, 7), ("give", 1, 0), ("give", 1, 1), ("give", 1, 2), ("ylast", 0, 1),
    ("xadd", 0, 3), ("xadd", 0, 4), ("zpass", 2, 0), ("p", 2, 0), ("xadd", 0, 5), ("give", 1, 3), ("give", 1, 4),
    ("give", 1, 5), ("give", 1, 6), ("give", 1, 7), ("p", 2, 1), ("sum", 1, 0), ("xypass", 0, 1), ("sum", 1, 1),
    ("xadd", 0, 6), ("sum", 1, 2), ("ylast", 0, 0), ("xadd", 0, 7), ("xypass", 0, 0), ("p", 2, 2), ("far", 2, 1),
    ("p", 2, 3), ("finy", 0, 1), ("sum", 1, 3), ("sum", 1, 4), ("sum", 1, 5), ("sum", 1, 6), ("sum", 1, 7),
    ("xadd", 1, 0), ("ypass", 1, 1, 0), ("ypass", 1, 0, 0), ("far", 2, 0), ("xadd", 1, 1), ("finx", 0, 1),
    ("ypass", 1, 0, 1), ("xadd", 1, 2), ("ypass", 1, 1, 1), ("p", 2, 4), ("p", 2, 5), ("xadd", 1, 4), ("finx", 0, 0),
    ("p", 2, 6), ("p", 2, 7), ("xypass", 1, 0), ("give", 2, 0), ("xadd", 1, 3), ("xadd", 1, 5), ("ylast", 1, 1),
    ("finy", 0, 0), ("give", 2, 1), ("give", 2, 2), ("give", 2, 3), ("give", 2, 4), ("give", 2, 5), ("xadd", 1, 6),
    ("give", 2, 6), ("give", 2, 7), ("ylast", 1, 0), ("xypass", 1, 1), ("give", 2, 8), ("give", 2, 9),
    ("give", 2, 10), ("give", 2, 11), ("give", 2, 12), ("give", 2, 13), ("xadd", 1, 7), ("give", 2, 14),
    ("give", 2, 15), ("sum", 2, 0), ("sum", 2, 1), ("sum", 2, 2), ("finy", 1, 1), ("sum", 2, 3), ("sum", 2, 4),
    ("sum", 2, 5), ("finx", 1, 1), ("finx", 1, 0), ("finy", 1, 0), ("top", 1), ("top", 0), ("sum", 2, 6),
    ("sum", 2, 7), ("sum", 2, 8), ("sum", 2, 9), ("xadd", 2, 0), ("sum", 2, 10), ("sum", 2, 11), ("ypass", 2, 0, 0),
    ("ypass", 2, 1, 0), ("sum", 2, 12), ("sum", 2, 13), ("sum", 2, 14), ("xadd", 2, 1), ("sum", 2, 15),
    ("ypass", 2, 0, 1), ("ypass", 2, 1, 1), ("xadd", 2, 2), ("xadd", 2, 3), ("xadd", 2, 4), ("xadd", 2, 5),
    ("xypass", 2, 0), ("ylast", 2, 1), ("xadd", 2, 6), ("ylast", 2, 0), ("xypass", 2, 1), ("xadd", 2, 7),
    ("finy", 2, 1), ("topa", 1), ("finy", 2, 0), ("topa", 0), ("finx", 2, 0), ("topb", 0), ("finx", 2, 1),
    ("topb", 1),
)

def split(value):
    high = value.astype(BF16)
    return high, (value - high.astype(F32)).astype(BF16)


def dot(a, b):
    return jnp.dot(a, b, preferred_element_type=F32)


def times(a_high, a_low, both, high):
    wide = dot(a_high, both)
    return wide[:, :HALF] + wide[:, HALF:] + dot(a_low, high)


def kernel(
    wanted_in, leaf_rhs_in, leaf_inv_in, off_blocks, top_rhs, top_inv, leaf_out, top_out,
    leaf_rhs, leaf_inv, wanted, found, meta,
    x_wide, x_pack, w, blocks, chain, give, s_wide, s_pack, y_wide, y_pack, xy_wide, xy_pack, far_wide, far_pack,
    last_wide, last_pack, rhs, inv, inv_high, inv_low,
    block_sem, top_sem, leaf_sem, meta_sem, az_s, az_r, ax_s, ax_r, core_s, core_r, y_s, y_r, xy_s, xy_r, x_s, x_r, x2_s, x2_r,
):
    row, col = lax.axis_index("prow"), lax.axis_index("pcol")
    z, xl = row // 2, row % 2
    xh, y, core = col // 8, (col // 2) % 4, col % 2

    def rows_at(dz, dx):
        return ((z + dz) % 4) * 2 + (xl + dx) % 2

    def at(dxh, dy, dcore):
        return ((xh + dxh) % 2) * 8 + ((y + dy) % 4) * 2 + (core + dcore) % 2

    x_near = (rows_at(0, 1), col)
    z_to = ((rows_at(1, 0), col), (rows_at(3, 0), col))
    other_core = (row, at(0, 0, 1))
    x_far = (row, at(1, 0, 0))
    y_to = ((row, at(0, 1, 0)), (row, at(0, 3, 0)))
    order = [rows_at(*d) for d in ((0, 0), (0, 1), (3, 0), (1, 0), (2, 0), (3, 1), (1, 1), (2, 1))]

    def send(src, dst, send_sem, recv_sem, device):
        return pltpu.make_async_remote_copy(
            src_ref=src, dst_ref=dst, send_sem=send_sem, recv_sem=recv_sem, device_id=device, device_id_type=MESH
        )

    def fetch(g):
        u = order[g % STEPS]
        return pltpu.make_async_copy(off_blocks.at[0, :, u], blocks.at[g % BUFS], block_sem.at[g % BUFS])

    left = lax.broadcasted_iota(jnp.int32, (1, HALF), 1) < 64

    def beside(first, second):
        return jnp.where(left, first, second)

    def turn(value):
        return pltpu.roll(value, 64, 1)

    def solution_piece(c, u, k):
        if PACKED[c]:
            return x_pack.at[NARROW.index(c), u, pl.ds(k * 128, 128)]
        return x_wide.at[u, k]

    def band(c, i, high):
        if not PACKED[c]:
            return s_wide, (i, pl.ds(CUT, REST) if high else pl.ds(0, CUT))
        pair, k = PAIRS.index(UNITS[i][:2]), UNITS[i][2]
        rows = pl.ds(2 * CUT_PACKED + k * REST_PACKED, REST_PACKED) if high else pl.ds(k * CUT_PACKED, CUT_PACKED)
        return s_pack, (NARROW.index(c), pair, rows)

    def arrived(c, kind, *index):
        wide, pack = {"y": (y_wide, y_pack), "xy": (xy_wide, xy_pack), "x": (far_wide, far_pack), "last": (last_wide, last_pack)}[kind]
        return (pack, (NARROW.index(c), *index)) if PACKED[c] else (wide, index)

    def add(c, i, high, kind, *index):
        need((kind, c, *index))
        ref, at_rows = band(c, i, high)
        got, at_got = arrived(c, kind, *index)
        ref[at_rows] = ref[at_rows] + got[at_got]

    fetch_leaf = [
        pltpu.make_async_copy(src, dst, leaf_sem.at[i])
        for i, (src, dst) in enumerate(((leaf_inv_in, leaf_inv), (leaf_rhs_in, leaf_rhs)))
    ]
    fetch_wanted = pltpu.make_async_copy(wanted_in, wanted, meta_sem.at[1])
    for copy in (*fetch_leaf, fetch_wanted):
        copy.start()

    barrier = pltpu.get_barrier_semaphore()
    partners = (x_near, *z_to, other_core, x_far, *y_to)
    for partner in partners:
        pl.semaphore_signal(barrier, inc=1, device_id=partner, device_id_type=MESH)

    for g in range(BUFS):
        fetch(g).start()
    fetch_rhs = pltpu.make_async_copy(top_rhs, rhs, top_sem.at[0])
    fetch_inv = pltpu.make_async_copy(top_inv, inv, top_sem.at[1])
    fetch_rhs.start()
    fetch_inv.start()

    for k in range(CHAINS):
        chain[k, NONE] = jnp.zeros((W2, HALF), F32)

    for copy in fetch_leaf:
        copy.wait()

    started, seen = {}, set()

    def put(key):
        if not started:
            pl.semaphore_wait(barrier, len(partners))
        started[key] = message(*key)
        started[key].start()

    def need(*keys):
        for key in keys:
            if key not in seen:
                seen.add(key)
                message(*key).wait_recv()

    def message(kind, c, j, k=0):
        if kind == "near":
            ref = solution_piece(c, order[0] if j == 0 else order[4], k)
            return send(ref, ref, ax_s.at[c, j, k], ax_r.at[c, j, k], x_near)
        if kind == "z":
            u = (order[0], order[0], order[2 + j], order[1], order[1], order[5 + j])[k]
            ref = solution_piece(c, u, (j, 1 - j, j, 0, 1, j)[k])
            return send(ref, ref, az_s.at[c, j, k], az_r.at[c, j, k], z_to[j])
        if kind == "core":
            into = s_pack.at[NARROW.index(c), j] if PACKED[c] else s_wide.at[j]
            return send(give.at[j], into, core_s.at[c, j], core_r.at[c, j], other_core)
        if kind == "y":
            i, high, index, sems, device = Y_SEND[j][k], False, (j, k), (y_s, y_r), y_to[j]
        elif kind == "xy":
            i, high, index, sems, device = XY_SEND[j][k], True, (j, k), (xy_s, xy_r), y_to[j]
        elif kind == "x":
            i, high, index, sems, device = X_SEND[j], True, (j,), (x_s, x_r), x_far
        else:
            i, high, index, sems, device = 12 + j, False, (j,), (x2_s, x2_r), x_far
        src, at_src = band(c, i, high)
        dst, at_dst = arrived(c, kind, *index)
        return send(src.at[at_src], dst.at[at_dst], sems[0].at[(c, *index)], sems[1].at[(c, *index)], device)

    def solve(v, cols):
        i_high, i_low = split(leaf_inv[0, v])
        r_high, r_low = split(leaf_rhs[0, v, :, cols])
        solved = times(i_high, i_low, jnp.concatenate([r_high, r_low], axis=1), r_high)
        leaf_out[0, v, :, cols] = solved
        return solved

    def leaf(c):
        if PACKED[c]:
            first, second = solve(0, slice(0, HALF)), solve(1, slice(0, HALF))
            second = turn(second)
            x_pack[0, row] = beside(first, second)
            x_pack[1, row] = beside(second, first)
        else:
            for v in range(2):
                x_wide[row, v] = solve(v, slice(HALF, 2 * HALF))

    def chains():
        fetch_wanted.wait()
        lane = lax.broadcasted_iota(jnp.int32, (8, HALF), 1)
        ask, limit, slots = lane - 32, jnp.full((8, HALF), 32, jnp.int32), []
        for step in range(STEPS):
            for v in range(2):
                for a in range(2):
                    slot, b = step * 4 + v * 2 + a, a * 16 + order[step] * 2 + v
                    ask = jnp.where(lane == b, wanted[b], ask)
                    limit = jnp.where(lane == b, slot, limit)
                    slots.append((slot, wanted[b]))
        before = jnp.full((8, HALF), NONE, jnp.int32)
        for slot, its_row in slots:
            before = jnp.where((ask == its_row) & (limit > slot), slot, before)
        found[...] = before
        copy = pltpu.make_async_copy(found, meta, meta_sem.at[0])
        copy.start()
        copy.wait()

    def own_x(c, v):
        put(("near", c, 0, v))

    def own_z(c):
        for j in range(2):
            for d in range(2):
                put(("z", c, d, j))

    def zpass(c, d):
        need(("z", c, d, 0))
        put(("z", c, d, 2))

    def near(c, j):
        need(("near", c, 0, j))
        for d in range(2):
            put(("z", c, d, 3 + j))

    def far(c, d):
        if FAR_BY[c] == Z_ONLY or (FAR_BY[c] == BOTH and d == 1):
            need(("z", c, d, 3 + d))
            put(("z", c, d, 5))
        else:
            need(("z", c, d, 2))
            put(("near", c, 1, d))

    def products(c, step):
        need(
            *(
                [],
                [("near", c, 0, 0), ("near", c, 0, 1)],
                [("z", c, 0, 0), ("z", c, 0, 1)],
                [("z", c, 1, 0), ("z", c, 1, 1)],
                [("z", c, 0, 2), ("z", c, 1, 2)],
                [("z", c, 0, 3), ("z", c, 0, 4)],
                [("z", c, 1, 3), ("z", c, 1, 4)],
                [
                    ("near", c, 1, d) if FAR_BY[c] == X_ONLY or (FAR_BY[c] == BOTH and d == 0) else ("z", c, d, 5)
                    for d in range(2)
                ],
            )[step]
        )
        g = c * STEPS + step
        u = order[step]
        fetch(g).wait()
        if PACKED[c]:
            k = NARROW.index(c)
            both = x_pack[k, u]
            turned = turn(both)
            columns = [beside(both, turned), beside(turned, both)]
            columns = columns if k == 0 else columns[::-1]
        else:
            columns = [x_wide[u, v] for v in range(2)]
        for v in range(2):
            high, low = split(columns[v])
            w[v, :, :HALF] = high
            w[v, :, HALF:] = low
        held = c % CHAINS

        def one(v, carry=0):
            for a in range(2):
                before = meta[0, a * 16 + u * 2 + v]
                for tile in range(2):
                    tall = slice(tile * 256, tile * 256 + 256)
                    b_high, b_low = split(blocks[g % BUFS, a, v, tall, :])
                    term = times(b_high, b_low, w[v], w[v, :, :HALF])
                    chain[held, step * 4 + v * 2 + a, tall, :] = term + chain[held, before, tall, :]
            return carry

        if c == 0:
            one(0), one(1)
        else:
            lax.fori_loop(0, 2, one, 0)
        if g + BUFS < PARTS * STEPS:
            fetch(g + BUFS).start()

    def total(c, i, its_core):
        dxh, dy = PAIRS[i] if PACKED[c] else UNITS[i][:2]
        first = ((xh + dxh) % 2) * 16 + ((y + dy) % 4) * 4 + its_core * 2
        if not PACKED[c]:
            return chain[c % CHAINS, meta[0, 32 + first + UNITS[i][2]]]
        pair = [chain[c % CHAINS, meta[0, 32 + first + e]] for e in range(2)]
        return beside(*(pair if NARROW.index(c) == 0 else pair[::-1]))

    def share_core(c, i):
        for before in range(c):
            if ("core", before, i) in started:
                started.pop(("core", before, i)).wait_send()
        give[i] = total(c, i, 1 - core)
        put(("core", c, i))

    def sum_core(c, i):
        need(("core", c, i))
        mine = total(c, i, core)
        if PACKED[c]:
            k = NARROW.index(c)
            s_pack[k, i] = s_pack[k, i] + mine
            units = [k for k in range(16) if UNITS[k][:2] == PAIRS[i]]
        else:
            s_wide[i] = s_wide[i] + mine
            units = [i]
        for unit in units:
            for d in range(2):
                if unit in Y_SEND[d][:4]:
                    put(("y", c, d, Y_SEND[d].index(unit)))
            if unit in X_SEND:
                put(("x", c, X_SEND.index(unit)))

    def y_add(c, i, js):
        for d in range(2):
            for j in js:
                if Y_ADD[d][j] == i:
                    add(c, i, False, "y", d, j)

    def pass_y(c, d, j):
        add(c, Y_ADD[d][j], False, "y", d, j)
        put(("y", c, d, 4 + j))

    def x_add(c, m):
        i = X_SEND[m] + 2
        add(c, i, True, "x", m)
        for d in range(2):
            if i in XY_SEND[d][:2]:
                put(("xy", c, d, XY_SEND[d].index(i)))

    def pass_xy(c, d):
        add(c, XY_ADD[d][0], True, "xy", d, 0)
        put(("xy", c, d, 2))

    def y_last(c, e):
        y_add(c, 12 + e, (2, 4))
        put(("last", c, e))

    def split_inv():
        fetch_rhs.wait()
        fetch_inv.wait()

        def one(i, carry):
            e, tall = i // 4, pl.ds(pl.multiple_of((i % 4) * 128, 128), 128)
            high, low = split(inv[e, tall, :])
            inv_high[e, tall, :] = high
            inv_low[e, tall, :] = low
            return carry

        lax.fori_loop(0, 8, one, 0)

    def finish_y(c, e):
        y_add(c, 14 + e, (3, 5))
        add(c, 14 + e, False, "last", e)

    def finish_xy(c, e):
        for d in range(2):
            for j in (1, 2):
                if XY_ADD[d][j] == 14 + e:
                    add(c, 14 + e, True, "xy", d, j)

    def block_times(e, below, right, value):
        high, low = split(value)
        both = jnp.concatenate([high, low], axis=1)
        return times(inv_high[e, below, right], inv_low[e, below, right], both, high)

    upper, lower, whole = slice(0, 256), slice(256, W2), slice(0, W2)
    narrow_cols, wide_cols = slice(0, HALF), slice(HALF, 2 * HALF)

    def top(e):
        pair = PAIRS.index((0, 0))
        sums = [s_pack[k, pair] for k in range(2)]
        value = rhs[e, :, narrow_cols] - (beside(*sums) if e == 0 else beside(*map(turn, sums)))
        top_out[e, upper, narrow_cols] = block_times(e, upper, upper, value[:256])
        top_out[e, lower, narrow_cols] = block_times(e, lower, whole, value)

    def top_upper(e):
        value = rhs[e, upper, wide_cols] - s_wide[14 + e, upper]
        top_out[e, upper, wide_cols] = block_times(e, upper, upper, value)
        top_out[e, lower, wide_cols] = block_times(e, lower, upper, value)

    def top_lower(e):
        value = rhs[e, lower, wide_cols] - s_wide[14 + e, lower]
        top_out[e, lower, wide_cols] = top_out[e, lower, wide_cols] + block_times(e, lower, lower, value)

    tasks = {
        "leaf": leaf, "ownx": own_x, "ownz": own_z, "zpass": zpass, "near": near, "far": far, "p": products, "inv": split_inv,
        "give": share_core, "sum": sum_core, "ypass": pass_y, "xadd": x_add, "xypass": pass_xy,
        "ylast": y_last, "finy": finish_y, "finx": finish_xy, "top": top, "topa": top_upper, "topb": top_lower,
        "chains": chains,
    }
    for name, *numbers in ORDER:
        tasks[name](*numbers)
    for copy in started.values():
        copy.wait_send()


def hand_over(leaf_in, top_in, leaf_out, top_out, sem):
    pieces = [(leaf_in.at[0, v], leaf_out.at[0, v]) for v in range(2)]
    pieces += [(top_in.at[e, half], top_out.at[e, half]) for e in range(2) for half in (pl.ds(0, 256), pl.ds(256, 256))]
    copies = [pltpu.make_async_copy(src, dst, sem.at[i]) for i, (src, dst) in enumerate(pieces)]
    for copy in copies:
        copy.start()
    for copy in copies:
        copy.wait()


def per_device(leaf_rhs, leaf_inverse, off_blocks, ancestor_rows, block_present, top_rhs, top_inverse):
    wanted = jnp.where(block_present != 0, ancestor_rows, -1).reshape(-1)
    anywhere = pl.BlockSpec(memory_space=pl.ANY)
    vmem = pl.BlockSpec(memory_space=pltpu.VMEM)
    dma = pltpu.SemaphoreType.DMA
    leaf, top = pl.pallas_call(
        kernel,
        out_shape=(pltpu.VMEM(leaf_rhs.shape, F32), pltpu.VMEM(top_rhs.shape, F32)),
        in_specs=[vmem] + [anywhere] * 5,
        out_specs=(vmem, vmem),
        scratch_shapes=[
            pltpu.VMEM(leaf_rhs.shape, F32),
            pltpu.VMEM(leaf_inverse.shape, F32),
            pltpu.SMEM((32,), jnp.int32),
            pltpu.VMEM((8, HALF), jnp.int32),
            pltpu.SMEM((8, HALF), jnp.int32),
            pltpu.VMEM((8, 2, W1, HALF), F32),
            pltpu.VMEM((2, 8, W1, HALF), F32),
            pltpu.VMEM((2, W1, 2 * HALF), BF16),
            pltpu.VMEM((BUFS, 2, 2, W2, W1), F32),
            pltpu.VMEM((CHAINS, NONE + 1, W2, HALF), F32),
            pltpu.VMEM((16, W2, HALF), F32),
            pltpu.VMEM((16, W2, HALF), F32),
            pltpu.VMEM((2, 8, W2, HALF), F32),
            pltpu.VMEM((2, 6, CUT, HALF), F32),
            pltpu.VMEM((2, 2, 6, CUT_PACKED, HALF), F32),
            pltpu.VMEM((2, 3, REST, HALF), F32),
            pltpu.VMEM((2, 2, 3, REST_PACKED, HALF), F32),
            pltpu.VMEM((8, REST, HALF), F32),
            pltpu.VMEM((2, 8, REST_PACKED, HALF), F32),
            pltpu.VMEM((2, CUT, HALF), F32),
            pltpu.VMEM((2, 2, CUT_PACKED, HALF), F32),
            pltpu.VMEM((2, W2, 2 * HALF), F32),
            pltpu.VMEM((2, W2, W2), F32),
            pltpu.VMEM((2, W2, W2), BF16),
            pltpu.VMEM((2, W2, W2), BF16),
            dma((BUFS,)),
            dma((2,)),
            dma((2,)),
            dma((2,)),
            *(dma((PARTS, *shape)) for shape in ((2, 6), (2, 2), (16,), (2, 6), (2, 3), (8,), (2,)) for _ in range(2)),
        ],
        compiler_params=pltpu.CompilerParams(
            collective_id=0, has_side_effects=True, vmem_limit_bytes=60 * 1024 * 1024
        ),
        cost_estimate=pl.CostEstimate(flops=7_500_000_000, bytes_accessed=40_000_000, transcendentals=0),
    )(pltpu.with_memory_space_constraint(wanted, pltpu.VMEM), leaf_rhs, leaf_inverse, off_blocks, top_rhs, top_inverse)
    return pl.pallas_call(
        hand_over,
        out_shape=(jax.ShapeDtypeStruct(leaf_rhs.shape, F32), jax.ShapeDtypeStruct(top_rhs.shape, F32)),
        in_specs=[vmem, vmem],
        out_specs=(anywhere, anywhere),
        scratch_shapes=[dma((6,))],
    )(*(pltpu.with_memory_space_constraint(value, pltpu.VMEM) for value in (leaf, top)))


def solution(mesh):
    return jax.shard_map(
        per_device,
        mesh=mesh,
        in_specs=(
            P("prow", "pcol", None, None),
            P("prow", "pcol", None, None),
            P("prow", None, None, "pcol", None, None),
            P("prow", None, None, "pcol"),
            P("prow", None, None, "pcol"),
            P(("prow", "pcol"), None, None),
            P(("prow", "pcol"), None, None),
        ),
        out_specs=(P("prow", "pcol", None, None), P(("prow", "pcol"), None, None)),
        check_vma=False,
    )
```

```python
import jax
import jax.numpy as jnp
from jax import lax
from jax.experimental import pallas as pl
from jax.experimental.pallas import tpu as pltpu
from jax.sharding import PartitionSpec as P

MESH = pl.DeviceIdType.MESH
F32, BF16 = jnp.float32, jnp.bfloat16
W1, W2, HALF = 256, 512, 128
STEPS = 8
BUFS = 3
CUT, REST = 288, 224
CUT_PACKED, REST_PACKED = 144, 112
NONE = 32
PACKED = (True, True, False)
PARTS = len(PACKED)
NARROW = tuple(c for c in range(PARTS) if PACKED[c])
CHAINS = 2
X_ONLY, BOTH, Z_ONLY = 0, 2, 1
FAR_BY = (2, 1, 1)

UNITS = (
    (1, 2, 0), (1, 2, 1), (0, 2, 0), (0, 2, 1),
    (1, 1, 1), (1, 3, 0), (0, 1, 1), (0, 3, 0),
    (1, 1, 0), (1, 3, 1), (0, 1, 0), (0, 3, 1),
    (1, 0, 0), (1, 0, 1), (0, 0, 0), (0, 0, 1),
)
PAIRS = ((1, 2), (0, 2), (1, 1), (1, 3), (0, 1), (0, 3), (1, 0), (0, 0))
Y_SEND = ((0, 2, 4, 6, 8, 10), (1, 3, 5, 7, 9, 11))
Y_ADD = ((8, 10, 13, 15, 12, 14), (9, 11, 12, 14, 13, 15))
X_SEND = (0, 1, 4, 5, 8, 9, 12, 13)
XY_SEND = ((2, 6, 10), (3, 7, 11))
XY_ADD = ((10, 15, 14), (11, 14, 15))


ORDER = (
    ("leaf", 0), ("ownx", 0, 1), ("ownz", 0), ("ownx", 0, 0), ("chains",), ("ownx", 1, 1), ("p", 0, 0),
    ("ownx", 1, 0), ("inv",), ("leaf", 2), ("zpass", 0, 0), ("zpass", 0, 1), ("near", 0, 1), ("near", 0, 0),
    ("p", 0, 1), ("p", 0, 2), ("p", 0, 3), ("far", 0, 0), ("p", 0, 4), ("ownx", 2, 1), ("ownx", 2, 0), ("far", 0, 1),
    ("ownz", 1), ("near", 1, 1), ("near", 1, 0), ("p", 0, 5), ("p", 0, 6), ("p", 0, 7), ("give", 0, 0),
    ("give", 0, 1), ("give", 0, 2), ("p", 1, 0), ("zpass", 1, 0), ("zpass", 1, 1), ("give", 0, 3), ("give", 0, 4),
    ("sum", 0, 0), ("give", 0, 5), ("give", 0, 6), ("give", 0, 7), ("sum", 0, 1), ("p", 1, 1), ("sum", 0, 2),
    ("sum", 0, 3), ("sum", 0, 4), ("far", 1, 0), ("far", 1, 1), ("ownz", 2), ("near", 2, 0), ("near", 2, 1),
    ("p", 1, 2), ("p", 1, 3), ("ypass", 0, 0, 0), ("xadd", 0, 0), ("ypass", 0, 1, 0), ("xadd", 0, 1), ("sum", 0, 5),
    ("sum", 0, 6), ("sum", 0, 7), ("p", 1, 4), ("ypass", 0, 0, 1), ("ypass", 0, 1, 1), ("p", 1, 5), ("xadd", 0, 2),
    ("p", 1, 6), ("p", 1, 7), ("give", 1, 0), ("ylast", 0, 1), ("xadd", 0, 5), ("give", 1, 1), ("zpass", 2, 1),
    ("xadd", 0, 3), ("give", 1, 2), ("ylast", 0, 0), ("give", 1, 3), ("give", 1, 4), ("zpass", 2, 0),
    ("xypass", 0, 1), ("xadd", 0, 4), ("give", 1, 5), ("xadd", 0, 6), ("give", 1, 6), ("give", 1, 7), ("sum", 1, 0),
    ("xypass", 0, 0), ("p", 2, 0), ("xadd", 0, 7), ("sum", 1, 1), ("sum", 1, 2), ("sum", 1, 3), ("p", 2, 1),
    ("p", 2, 2), ("far", 2, 0), ("finy", 0, 1), ("p", 2, 3), ("finy", 0, 0), ("ypass", 1, 0, 0), ("finx", 0, 1),
    ("xadd", 1, 0), ("sum", 1, 4), ("sum", 1, 5), ("sum", 1, 6), ("ypass", 1, 1, 0), ("sum", 1, 7), ("far", 2, 1),
    ("finx", 0, 0), ("xadd", 1, 1), ("ypass", 1, 0, 1), ("ypass", 1, 1, 1), ("xadd", 1, 2), ("p", 2, 4), ("p", 2, 5),
    ("ylast", 1, 0), ("p", 2, 6), ("xadd", 1, 3), ("p", 2, 7), ("give", 2, 0), ("ylast", 1, 1), ("xadd", 1, 4),
    ("give", 2, 1), ("xypass", 1, 0), ("xadd", 1, 5), ("xypass", 1, 1), ("xadd", 1, 6), ("give", 2, 2),
    ("give", 2, 3), ("give", 2, 4), ("give", 2, 5), ("xadd", 1, 7), ("give", 2, 6), ("give", 2, 7), ("give", 2, 8),
    ("sum", 2, 0), ("give", 2, 9), ("give", 2, 10), ("sum", 2, 1), ("give", 2, 11), ("give", 2, 12), ("finy", 1, 0),
    ("give", 2, 13), ("sum", 2, 2), ("sum", 2, 3), ("give", 2, 14), ("give", 2, 15), ("sum", 2, 4), ("sum", 2, 5),
    ("sum", 2, 6), ("finy", 1, 1), ("sum", 2, 7), ("finx", 1, 1), ("finx", 1, 0), ("sum", 2, 8), ("top", 0),
    ("sum", 2, 9), ("sum", 2, 10), ("sum", 2, 11), ("sum", 2, 12), ("top", 1), ("sum", 2, 13), ("sum", 2, 14),
    ("sum", 2, 15), ("ypass", 2, 0, 0), ("ypass", 2, 1, 0), ("xadd", 2, 0), ("xadd", 2, 1), ("ypass", 2, 0, 1),
    ("ypass", 2, 1, 1), ("xadd", 2, 2), ("xadd", 2, 3), ("xadd", 2, 4), ("xadd", 2, 5), ("ylast", 2, 0),
    ("ylast", 2, 1), ("xadd", 2, 6), ("xypass", 2, 0), ("xypass", 2, 1), ("xadd", 2, 7), ("finy", 2, 0), ("topa", 0),
    ("finy", 2, 1), ("topa", 1), ("finx", 2, 0), ("topb", 0), ("finx", 2, 1), ("topb", 1),
)


def split(value):
    high = value.astype(BF16)
    return high, (value - high.astype(F32)).astype(BF16)


def dot(a, b):
    return jnp.dot(a, b, preferred_element_type=F32)


def times(a_high, a_low, both, high):
    wide = dot(a_high, both)
    return wide[:, :HALF] + wide[:, HALF:] + dot(a_low, high)


def kernel(
    wanted_in, leaf_rhs_in, leaf_inv_in, off_blocks, top_rhs, top_inv, leaf_out, top_out,
    leaf_rhs, leaf_inv, wanted, found, meta,
    x_wide, x_pack, w, blocks, chain, give, s_wide, s_pack, y_wide, y_pack, xy_wide, xy_pack, far_wide, far_pack,
    last_wide, last_pack, rhs, inv, inv_high, inv_low,
    block_sem, top_sem, leaf_sem, meta_sem, az_s, az_r, ax_s, ax_r, core_s, core_r, y_s, y_r, xy_s, xy_r, x_s, x_r, x2_s, x2_r,
):
    row, col = lax.axis_index("prow"), lax.axis_index("pcol")
    z, xl = row // 2, row % 2
    xh, y, core = col // 8, (col // 2) % 4, col % 2

    def rows_at(dz, dx):
        return ((z + dz) % 4) * 2 + (xl + dx) % 2

    def at(dxh, dy, dcore):
        return ((xh + dxh) % 2) * 8 + ((y + dy) % 4) * 2 + (core + dcore) % 2

    x_near = (rows_at(0, 1), col)
    z_to = ((rows_at(1, 0), col), (rows_at(3, 0), col))
    other_core = (row, at(0, 0, 1))
    x_far = (row, at(1, 0, 0))
    y_to = ((row, at(0, 1, 0)), (row, at(0, 3, 0)))
    order = [rows_at(*d) for d in ((0, 0), (0, 1), (3, 0), (1, 0), (2, 0), (3, 1), (1, 1), (2, 1))]

    def send(src, dst, send_sem, recv_sem, device):
        return pltpu.make_async_remote_copy(
            src_ref=src, dst_ref=dst, send_sem=send_sem, recv_sem=recv_sem, device_id=device, device_id_type=MESH
        )

    def fetch(g):
        u = order[g % STEPS]
        return pltpu.make_async_copy(off_blocks.at[0, :, u], blocks.at[g % BUFS], block_sem.at[g % BUFS])

    left = lax.broadcasted_iota(jnp.int32, (1, HALF), 1) < 64

    def beside(first, second):
        return jnp.where(left, first, second)

    def turn(value):
        return pltpu.roll(value, 64, 1)

    def solution_piece(c, u, k):
        if PACKED[c]:
            return x_pack.at[NARROW.index(c), u, pl.ds(k * 128, 128)]
        return x_wide.at[u, k]

    def band(c, i, high):
        if not PACKED[c]:
            return s_wide, (i, pl.ds(CUT, REST) if high else pl.ds(0, CUT))
        pair, k = PAIRS.index(UNITS[i][:2]), UNITS[i][2]
        rows = pl.ds(2 * CUT_PACKED + k * REST_PACKED, REST_PACKED) if high else pl.ds(k * CUT_PACKED, CUT_PACKED)
        return s_pack, (NARROW.index(c), pair, rows)

    def arrived(c, kind, *index):
        wide, pack = {"y": (y_wide, y_pack), "xy": (xy_wide, xy_pack), "x": (far_wide, far_pack), "last": (last_wide, last_pack)}[kind]
        return (pack, (NARROW.index(c), *index)) if PACKED[c] else (wide, index)

    def add(c, i, high, kind, *index):
        need((kind, c, *index))
        ref, at_rows = band(c, i, high)
        got, at_got = arrived(c, kind, *index)
        ref[at_rows] = ref[at_rows] + got[at_got]

    fetch_leaf = [
        pltpu.make_async_copy(src, dst, leaf_sem.at[i])
        for i, (src, dst) in enumerate(((leaf_inv_in, leaf_inv), (leaf_rhs_in, leaf_rhs)))
    ]
    fetch_wanted = pltpu.make_async_copy(wanted_in, wanted, meta_sem.at[1])
    for copy in (*fetch_leaf, fetch_wanted):
        copy.start()

    barrier = pltpu.get_barrier_semaphore()
    partners = (x_near, *z_to, other_core, x_far, *y_to)
    for partner in partners:
        pl.semaphore_signal(barrier, inc=1, device_id=partner, device_id_type=MESH)

    for g in range(BUFS):
        fetch(g).start()
    fetch_rhs = pltpu.make_async_copy(top_rhs, rhs, top_sem.at[0])
    fetch_inv = pltpu.make_async_copy(top_inv, inv, top_sem.at[1])
    fetch_rhs.start()
    fetch_inv.start()

    for k in range(CHAINS):
        chain[k, NONE] = jnp.zeros((W2, HALF), F32)

    for copy in fetch_leaf:
        copy.wait()

    started, seen = {}, set()

    def put(key):
        if not started:
            pl.semaphore_wait(barrier, len(partners))
        started[key] = message(*key)
        started[key].start()

    def need(*keys):
        for key in keys:
            if key not in seen:
                seen.add(key)
                message(*key).wait_recv()

    def message(kind, c, j, k=0):
        if kind == "near":
            ref = solution_piece(c, order[0] if j == 0 else order[4], k)
            return send(ref, ref, ax_s.at[c, j, k], ax_r.at[c, j, k], x_near)
        if kind == "z":
            u = (order[0], order[0], order[2 + j], order[1], order[1], order[5 + j])[k]
            ref = solution_piece(c, u, (j, 1 - j, j, 0, 1, j)[k])
            return send(ref, ref, az_s.at[c, j, k], az_r.at[c, j, k], z_to[j])
        if kind == "core":
            into = s_pack.at[NARROW.index(c), j] if PACKED[c] else s_wide.at[j]
            return send(give.at[j], into, core_s.at[c, j], core_r.at[c, j], other_core)
        if kind == "y":
            i, high, index, sems, device = Y_SEND[j][k], False, (j, k), (y_s, y_r), y_to[j]
        elif kind == "xy":
            i, high, index, sems, device = XY_SEND[j][k], True, (j, k), (xy_s, xy_r), y_to[j]
        elif kind == "x":
            i, high, index, sems, device = X_SEND[j], True, (j,), (x_s, x_r), x_far
        else:
            i, high, index, sems, device = 12 + j, False, (j,), (x2_s, x2_r), x_far
        src, at_src = band(c, i, high)
        dst, at_dst = arrived(c, kind, *index)
        return send(src.at[at_src], dst.at[at_dst], sems[0].at[(c, *index)], sems[1].at[(c, *index)], device)

    def solve(v, cols):
        i_high, i_low = split(leaf_inv[0, v])
        r_high, r_low = split(leaf_rhs[0, v, :, cols])
        solved = times(i_high, i_low, jnp.concatenate([r_high, r_low], axis=1), r_high)
        leaf_out[0, v, :, cols] = solved
        return solved

    def leaf(c):
        if PACKED[c]:
            first, second = solve(0, slice(0, HALF)), solve(1, slice(0, HALF))
            second = turn(second)
            x_pack[0, row] = beside(first, second)
            x_pack[1, row] = beside(second, first)
        else:
            for v in range(2):
                x_wide[row, v] = solve(v, slice(HALF, 2 * HALF))

    def chains():
        fetch_wanted.wait()
        lane = lax.broadcasted_iota(jnp.int32, (8, HALF), 1)
        ask, limit, slots = lane - 32, jnp.full((8, HALF), 32, jnp.int32), []
        for step in range(STEPS):
            for v in range(2):
                for a in range(2):
                    slot, b = step * 4 + v * 2 + a, a * 16 + order[step] * 2 + v
                    ask = jnp.where(lane == b, wanted[b], ask)
                    limit = jnp.where(lane == b, slot, limit)
                    slots.append((slot, wanted[b]))
        before = jnp.full((8, HALF), NONE, jnp.int32)
        for slot, its_row in slots:
            before = jnp.where((ask == its_row) & (limit > slot), slot, before)
        found[...] = before
        copy = pltpu.make_async_copy(found, meta, meta_sem.at[0])
        copy.start()
        copy.wait()

    def own_x(c, v):
        put(("near", c, 0, v))

    def own_z(c):
        for j in range(2):
            for d in range(2):
                put(("z", c, d, j))

    def zpass(c, d):
        need(("z", c, d, 0))
        put(("z", c, d, 2))

    def near(c, j):
        need(("near", c, 0, j))
        for d in range(2):
            put(("z", c, d, 3 + j))

    def far(c, d):
        if FAR_BY[c] == Z_ONLY or (FAR_BY[c] == BOTH and d == 1):
            need(("z", c, d, 3 + d))
            put(("z", c, d, 5))
        else:
            need(("z", c, d, 2))
            put(("near", c, 1, d))

    def products(c, step):
        need(
            *(
                [],
                [("near", c, 0, 0), ("near", c, 0, 1)],
                [("z", c, 0, 0), ("z", c, 0, 1)],
                [("z", c, 1, 0), ("z", c, 1, 1)],
                [("z", c, 0, 2), ("z", c, 1, 2)],
                [("z", c, 0, 3), ("z", c, 0, 4)],
                [("z", c, 1, 3), ("z", c, 1, 4)],
                [
                    ("near", c, 1, d) if FAR_BY[c] == X_ONLY or (FAR_BY[c] == BOTH and d == 0) else ("z", c, d, 5)
                    for d in range(2)
                ],
            )[step]
        )
        g = c * STEPS + step
        u = order[step]
        fetch(g).wait()
        if PACKED[c]:
            k = NARROW.index(c)
            both = x_pack[k, u]
            turned = turn(both)
            columns = [beside(both, turned), beside(turned, both)]
            columns = columns if k == 0 else columns[::-1]
        else:
            columns = [x_wide[u, v] for v in range(2)]
        for v in range(2):
            high, low = split(columns[v])
            w[v, :, :HALF] = high
            w[v, :, HALF:] = low
        held = c % CHAINS

        def one(v, carry=0):
            for a in range(2):
                before = meta[0, a * 16 + u * 2 + v]
                for tile in range(2):
                    tall = slice(tile * 256, tile * 256 + 256)
                    b_high, b_low = split(blocks[g % BUFS, a, v, tall, :])
                    term = times(b_high, b_low, w[v], w[v, :, :HALF])
                    chain[held, step * 4 + v * 2 + a, tall, :] = term + chain[held, before, tall, :]
            return carry

        if c == 0:
            one(0), one(1)
        else:
            lax.fori_loop(0, 2, one, 0)
        if g + BUFS < PARTS * STEPS:
            fetch(g + BUFS).start()

    def total(c, i, its_core):
        dxh, dy = PAIRS[i] if PACKED[c] else UNITS[i][:2]
        first = ((xh + dxh) % 2) * 16 + ((y + dy) % 4) * 4 + its_core * 2
        if not PACKED[c]:
            return chain[c % CHAINS, meta[0, 32 + first + UNITS[i][2]]]
        pair = [chain[c % CHAINS, meta[0, 32 + first + e]] for e in range(2)]
        return beside(*(pair if NARROW.index(c) == 0 else pair[::-1]))

    def share_core(c, i):
        for before in range(c):
            if ("core", before, i) in started:
                started.pop(("core", before, i)).wait_send()
        give[i] = total(c, i, 1 - core)
        put(("core", c, i))

    def sum_core(c, i):
        need(("core", c, i))
        mine = total(c, i, core)
        if PACKED[c]:
            k = NARROW.index(c)
            s_pack[k, i] = s_pack[k, i] + mine
            units = [k for k in range(16) if UNITS[k][:2] == PAIRS[i]]
        else:
            s_wide[i] = s_wide[i] + mine
            units = [i]
        for unit in units:
            for d in range(2):
                if unit in Y_SEND[d][:4]:
                    put(("y", c, d, Y_SEND[d].index(unit)))
            if unit in X_SEND:
                put(("x", c, X_SEND.index(unit)))

    def y_add(c, i, js):
        for d in range(2):
            for j in js:
                if Y_ADD[d][j] == i:
                    add(c, i, False, "y", d, j)

    def pass_y(c, d, j):
        add(c, Y_ADD[d][j], False, "y", d, j)
        put(("y", c, d, 4 + j))

    def x_add(c, m):
        i = X_SEND[m] + 2
        add(c, i, True, "x", m)
        for d in range(2):
            if i in XY_SEND[d][:2]:
                put(("xy", c, d, XY_SEND[d].index(i)))

    def pass_xy(c, d):
        add(c, XY_ADD[d][0], True, "xy", d, 0)
        put(("xy", c, d, 2))

    def y_last(c, e):
        y_add(c, 12 + e, (2, 4))
        put(("last", c, e))

    def split_inv():
        fetch_rhs.wait()
        fetch_inv.wait()

        def one(i, carry):
            e, tall = i // 4, pl.ds(pl.multiple_of((i % 4) * 128, 128), 128)
            high, low = split(inv[e, tall, :])
            inv_high[e, tall, :] = high
            inv_low[e, tall, :] = low
            return carry

        lax.fori_loop(0, 8, one, 0)

    def finish_y(c, e):
        y_add(c, 14 + e, (3, 5))
        add(c, 14 + e, False, "last", e)

    def finish_xy(c, e):
        for d in range(2):
            for j in (1, 2):
                if XY_ADD[d][j] == 14 + e:
                    add(c, 14 + e, True, "xy", d, j)

    def block_times(e, below, right, value):
        high, low = split(value)
        both = jnp.concatenate([high, low], axis=1)
        return times(inv_high[e, below, right], inv_low[e, below, right], both, high)

    upper, lower, whole = slice(0, 256), slice(256, W2), slice(0, W2)
    narrow_cols, wide_cols = slice(0, HALF), slice(HALF, 2 * HALF)

    def top(e):
        pair = PAIRS.index((0, 0))
        sums = [s_pack[k, pair] for k in range(2)]
        value = rhs[e, :, narrow_cols] - (beside(*sums) if e == 0 else beside(*map(turn, sums)))
        top_out[e, upper, narrow_cols] = block_times(e, upper, upper, value[:256])
        top_out[e, lower, narrow_cols] = block_times(e, lower, whole, value)

    def top_upper(e):
        value = rhs[e, upper, wide_cols] - s_wide[14 + e, upper]
        top_out[e, upper, wide_cols] = block_times(e, upper, upper, value)
        top_out[e, lower, wide_cols] = block_times(e, lower, upper, value)

    def top_lower(e):
        value = rhs[e, lower, wide_cols] - s_wide[14 + e, lower]
        top_out[e, lower, wide_cols] = top_out[e, lower, wide_cols] + block_times(e, lower, lower, value)

    tasks = {
        "leaf": leaf, "ownx": own_x, "ownz": own_z, "zpass": zpass, "near": near, "far": far, "p": products, "inv": split_inv,
        "give": share_core, "sum": sum_core, "ypass": pass_y, "xadd": x_add, "xypass": pass_xy,
        "ylast": y_last, "finy": finish_y, "finx": finish_xy, "top": top, "topa": top_upper, "topb": top_lower,
        "chains": chains,
    }
    for name, *numbers in ORDER:
        tasks[name](*numbers)
    for copy in started.values():
        copy.wait_send()


def hand_over(leaf_in, top_in, leaf_out, top_out, sem):
    pieces = [(leaf_in.at[0, v], leaf_out.at[0, v]) for v in range(2)]
    pieces += [(top_in.at[e, half], top_out.at[e, half]) for e in range(2) for half in (pl.ds(0, 256), pl.ds(256, 256))]
    copies = [pltpu.make_async_copy(src, dst, sem.at[i]) for i, (src, dst) in enumerate(pieces)]
    for copy in copies:
        copy.start()
    for copy in copies:
        copy.wait()


def per_device(leaf_rhs, leaf_inverse, off_blocks, ancestor_rows, block_present, top_rhs, top_inverse):
    wanted = jnp.where(block_present != 0, ancestor_rows, -1).reshape(-1)
    anywhere = pl.BlockSpec(memory_space=pl.ANY)
    vmem = pl.BlockSpec(memory_space=pltpu.VMEM)
    dma = pltpu.SemaphoreType.DMA
    leaf, top = pl.pallas_call(
        kernel,
        out_shape=(pltpu.VMEM(leaf_rhs.shape, F32), pltpu.VMEM(top_rhs.shape, F32)),
        in_specs=[vmem] + [anywhere] * 5,
        out_specs=(vmem, vmem),
        scratch_shapes=[
            pltpu.VMEM(leaf_rhs.shape, F32),
            pltpu.VMEM(leaf_inverse.shape, F32),
            pltpu.SMEM((32,), jnp.int32),
            pltpu.VMEM((8, HALF), jnp.int32),
            pltpu.SMEM((8, HALF), jnp.int32),
            pltpu.VMEM((8, 2, W1, HALF), F32),
            pltpu.VMEM((2, 8, W1, HALF), F32),
            pltpu.VMEM((2, W1, 2 * HALF), BF16),
            pltpu.VMEM((BUFS, 2, 2, W2, W1), F32),
            pltpu.VMEM((CHAINS, NONE + 1, W2, HALF), F32),
            pltpu.VMEM((16, W2, HALF), F32),
            pltpu.VMEM((16, W2, HALF), F32),
            pltpu.VMEM((2, 8, W2, HALF), F32),
            pltpu.VMEM((2, 6, CUT, HALF), F32),
            pltpu.VMEM((2, 2, 6, CUT_PACKED, HALF), F32),
            pltpu.VMEM((2, 3, REST, HALF), F32),
            pltpu.VMEM((2, 2, 3, REST_PACKED, HALF), F32),
            pltpu.VMEM((8, REST, HALF), F32),
            pltpu.VMEM((2, 8, REST_PACKED, HALF), F32),
            pltpu.VMEM((2, CUT, HALF), F32),
            pltpu.VMEM((2, 2, CUT_PACKED, HALF), F32),
            pltpu.VMEM((2, W2, 2 * HALF), F32),
            pltpu.VMEM((2, W2, W2), F32),
            pltpu.VMEM((2, W2, W2), BF16),
            pltpu.VMEM((2, W2, W2), BF16),
            dma((BUFS,)),
            dma((2,)),
            dma((2,)),
            dma((2,)),
            *(dma((PARTS, *shape)) for shape in ((2, 6), (2, 2), (16,), (2, 6), (2, 3), (8,), (2,)) for _ in range(2)),
        ],
        compiler_params=pltpu.CompilerParams(
            collective_id=0, has_side_effects=True, vmem_limit_bytes=60 * 1024 * 1024
        ),
        cost_estimate=pl.CostEstimate(flops=7_500_000_000, bytes_accessed=40_000_000, transcendentals=0),
    )(pltpu.with_memory_space_constraint(wanted, pltpu.VMEM), leaf_rhs, leaf_inverse, off_blocks, top_rhs, top_inverse)
    return pl.pallas_call(
        hand_over,
        out_shape=(jax.ShapeDtypeStruct(leaf_rhs.shape, F32), jax.ShapeDtypeStruct(top_rhs.shape, F32)),
        in_specs=[vmem, vmem],
        out_specs=(anywhere, anywhere),
        scratch_shapes=[dma((6,))],
    )(*(pltpu.with_memory_space_constraint(value, pltpu.VMEM) for value in (leaf, top)))


def solution(mesh):
    return jax.shard_map(
        per_device,
        mesh=mesh,
        in_specs=(
            P("prow", "pcol", None, None),
            P("prow", "pcol", None, None),
            P("prow", None, None, "pcol", None, None),
            P("prow", None, None, "pcol"),
            P("prow", None, None, "pcol"),
            P(("prow", "pcol"), None, None),
            P(("prow", "pcol"), None, None),
        ),
        out_specs=(P("prow", "pcol", None, None), P(("prow", "pcol"), None, None)),
        check_vma=False,
    )
```
